256 devices in a mesh: ctx: 32 (over y_lo, z, core), head: 8 (over y_hi, x).
Axes of the slice: x: 4, y: 4 (y_hi: 2, y_lo: 2; y = y_hi * 2 + y_lo), z: 8, core: 2. Of those that a mesh axis runs over, the one named last changes fastest.
Arguments:
- queries: bfloat16 [4096, 2048], P('ctx', 'head'), may hold values from -6 to 6
- key_states: bfloat16 [4096, 2048], P('ctx', 'head'), may hold values from -6 to 6
- value_states: bfloat16 [4096, 2048], P('ctx', 'head'), may hold values from -6 to 6
- memory_keys: bfloat16 [1024, 2048], P('ctx', 'head'), may hold values from -6 to 6
- memory_values: bfloat16 [1024, 2048], P('ctx', 'head'), may hold values from -6 to 6
- memory_length: int32 [32], replicated, may hold values from 256 to 1024, as said below
- block_mask: int32 [32, 32], replicated, may hold values from 0 to 1, as said below
- out_weight: bfloat16 [2048, 4096], P('head'), may hold values from -0.125 to 0.125
- out_grad: bfloat16 [4096, 4096], P('ctx'), may hold values from -6 to 6
Outputs:
- layer_out: bfloat16 [4096, 4096], P('ctx', 'head')
- grad_weight: bfloat16 [2048, 4096], P('head', 'ctx')
- grad_queries: bfloat16 [4096, 2048], P('ctx', 'head')
- grad_keys: bfloat16 [4096, 2048], P('ctx', 'head')
- grad_values: bfloat16 [4096, 2048], P('ctx', 'head')
The draws below stay inside these ranges and needn't reach their ends.
Inputs may be any that keep to these rules, and one draw needn't show every extreme that they name: `memory_length`: at least 256; some block sees all 1024. `block_mask`: 0 or 1; every diagonal entry is 1.
All inputs are finite; a program needn't handle non-finite values.
Results may differ from the reference program's by a relative error of at most 0.03.
Values may be sent and summed in bfloat16 or wider, within the bound.
A program may use at most 128 MiB of HBM per device.

```python
import math
import jax
import jax.numpy as jnp
from jax import lax

D = 4096
HEADS = 16
HD = 128
BLK = 128
MEM = 1024
TOKENS = 4096
HH = 2048
N_BLK = 32


def draw_queries(key, part):
    key = jax.random.fold_in(key, 1)
    base = jnp.clip(jax.random.normal(key, (TOKENS, HEADS * HD), jnp.float32), -5.5, 5.5)
    return base.astype(jnp.bfloat16)


def draw_key_states(key, part):
    key = jax.random.fold_in(key, 2)
    base = jnp.clip(jax.random.normal(key, (TOKENS, HEADS * HD), jnp.float32), -5.5, 5.5)
    return base.astype(jnp.bfloat16)


def draw_memory_length(key, part):
    key = jax.random.fold_in(key, 3)
    length_key, pick_key = jax.random.split(key)
    lengths = jax.random.randint(length_key, (N_BLK,), MEM // 4, MEM + 1)
    full_block = jax.random.randint(pick_key, (), 0, N_BLK)
    return jnp.where(jnp.arange(N_BLK) == full_block, MEM, lengths).astype(jnp.int32)


def draw_block_mask(key, part):
    key = jax.random.fold_in(key, 4)
    level_key, pick_key = jax.random.split(key)
    level = jax.random.randint(level_key, (N_BLK,), 0, 4)
    pick = jax.random.randint(pick_key, (N_BLK, N_BLK), 0, 8)
    mask = (pick < level[:, None] + level[None, :]).astype(jnp.int32)
    diagonal = jnp.arange(N_BLK)[:, None] == jnp.arange(N_BLK)[None, :]
    return jnp.where(diagonal, 1, mask).astype(jnp.int32)


def with_spikes(entries, stream_key, source, target, blocks, factor):
    def block_of(position):
        return (jnp.arange(entries.shape[position]) // (entries.shape[position] // blocks)).reshape((-1,) + (1,) * (entries.ndim - 1 - position))

    first = jax.random.permutation(stream_key, blocks)[block_of(target)]
    second = (block_of(target) + blocks // 2) % blocks
    return jnp.where((block_of(source) == first) | (block_of(source) == second), factor * entries, entries)


def level_of(key, shape, shards, smallest, high):
    level, own = 1.0, jax.random.fold_in(key, 6)
    for dim, parts in shards:
        steps = jnp.exp(jax.random.uniform(jax.random.fold_in(own, dim), (parts,), jnp.float32, smallest / len(shards), high / len(shards)))
        level = level * jnp.repeat(steps, shape[dim] // parts).reshape([-1 if axis == dim else 1 for axis in range(len(shape))])
    return level


def bell_draw(own_key, dims, scale, bound, shards=(), kind=jnp.bfloat16):
    values = scale * jax.random.normal(own_key, dims, jnp.float32)
    if shards:
        values = values * level_of(own_key, dims, shards, -0.22, 0.18)
    return jnp.clip(values, -bound, bound).astype(kind)


def heavy_noise(own_key, dims, spread, bound, cuts, heavy, held_as=jnp.bfloat16):
    result = spread * jax.random.normal(own_key, dims, jnp.float32)
    if cuts:
        result = result * level_of(own_key, dims, cuts, -0.22, 0.18)
    return jnp.clip(with_spikes(result, jax.random.fold_in(own_key, 3), *heavy), -bound, bound).astype(held_as)


def setup_inputs(seed: int = 0) -> dict:
    seeds = jax.random.split(jax.random.key(seed), 10)
    return {
        "queries": draw_queries(jax.random.fold_in(seeds[9], 71), 0),
        "key_states": draw_key_states(jax.random.fold_in(seeds[9], 71), 0),
        "value_states": bell_draw(seeds[2], (TOKENS, HH), 1.0, 6.0, ((0, 32), (1, 8))),
        "memory_keys": bell_draw(seeds[3], (MEM, HH), 1.0, 6.0, ((0, 32), (1, 8))),
        "memory_values": bell_draw(seeds[4], (MEM, HH), 1.0, 6.0, ((0, 32), (1, 8))),
        "memory_length": draw_memory_length(jax.random.fold_in(seeds[9], 71), 0),
        "block_mask": draw_block_mask(jax.random.fold_in(seeds[9], 71), 0),
        "out_weight": bell_draw(seeds[7], (HH, D), HH ** -0.5, 0.125, ((0, 8),)),
        "out_grad": heavy_noise(seeds[8], (TOKENS, D), 1.0, 6.0, ((0, 32),), (0, 1, 32, 2.75)),
    }


def split_heads(values):
    return values.reshape(values.shape[0], HEADS, HD).transpose(1, 0, 2)

def merge_heads(values):
    return values.transpose(1, 0, 2).reshape(values.shape[1], HEADS * HD)

def reference(queries, key_states, value_states, memory_keys, memory_values, memory_length, block_mask, out_weight, out_grad):
    scale = 1.0 / math.sqrt(HD)
    tok_block = (jnp.arange(TOKENS) // BLK).astype(jnp.int32)
    seq_allow = block_mask[tok_block][:, tok_block] > 0
    mem_allow = jnp.arange(MEM)[None, :] < memory_length[tok_block][:, None]
    allow = jnp.concatenate([mem_allow, seq_allow], axis=1)
    all_keys = split_heads(jnp.concatenate([memory_keys, key_states], axis=0))
    all_values = split_heads(jnp.concatenate([memory_values, value_states], axis=0))
    query_heads = split_heads(queries)

    def scores_of(query, keys):
        scores = jnp.dot(query, keys.T, preferred_element_type=jnp.float32) * scale
        return jnp.where(allow, scores, -jnp.inf)

    def forward(operands):
        query, keys, values = operands
        scores = scores_of(query, keys)
        top = lax.optimization_barrier(jnp.max(scores, axis=1, keepdims=True))
        lse = top + jnp.log(lax.optimization_barrier(jnp.sum(jnp.exp(scores - top), axis=1, keepdims=True)))
        probs = jnp.exp(scores - lse)
        out = jnp.dot(probs, values.astype(jnp.float32), precision=lax.Precision.HIGHEST, preferred_element_type=jnp.float32).astype(jnp.bfloat16)
        return (out, lse[:, 0])
    att_heads, lse_heads = lax.map(forward, (query_heads, all_keys, all_values))
    attended = merge_heads(att_heads)
    layer_out = jnp.dot(attended, out_weight, preferred_element_type=jnp.float32).astype(jnp.bfloat16)
    grad_weight = jnp.dot(attended.T, out_grad, preferred_element_type=jnp.float32).astype(jnp.bfloat16)
    grad_att = jnp.dot(out_grad, out_weight.T, preferred_element_type=jnp.float32).astype(jnp.bfloat16)
    grad_heads = split_heads(grad_att)

    def backward(operands):
        query, keys, values, output, grad_out, lse = operands
        scores = scores_of(query, keys)
        probs = jnp.exp(scores - lse[:, None])
        delta = lax.optimization_barrier(jnp.sum(grad_out.astype(jnp.float32) * output.astype(jnp.float32), axis=1))
        grad_probs = jnp.dot(grad_out, values.T, preferred_element_type=jnp.float32)
        grad_scores = (probs * (grad_probs - delta[:, None])).astype(jnp.bfloat16)
        grad_q = jnp.dot(grad_scores, keys, preferred_element_type=jnp.float32) * scale
        grad_k = jnp.dot(grad_scores.T, query, preferred_element_type=jnp.float32) * scale
        grad_v = jnp.dot(probs.astype(jnp.bfloat16).T, grad_out, preferred_element_type=jnp.float32)
        return (grad_q.astype(jnp.bfloat16), grad_k[MEM:].astype(jnp.bfloat16), grad_v[MEM:].astype(jnp.bfloat16))
    grad_q, grad_k, grad_v = lax.map(backward, (query_heads, all_keys, all_values, att_heads, grad_heads, lse_heads))
    return (layer_out, grad_weight, merge_heads(grad_q), merge_heads(grad_k), merge_heads(grad_v))
```

```python
import functools
import math

import jax
import jax.numpy as jnp
from jax import lax
from jax.experimental import pallas as pl
from jax.experimental.pallas import tpu as pltpu
from jax.sharding import PartitionSpec as P

HD = 128
BLK = 128
NZ = 8
F32 = jnp.float32
BF16 = jnp.bfloat16
MESH = pl.DeviceIdType.MESH
LOG2E = 1.4426950408889634

OFFSET = (0, -1, 1, -2, 2, -3, 3, 4)
SLOT_OF = {off % NZ: slot for slot, off in enumerate(OFFSET)}

K0, V0, MK0, MV0, ROWS1 = 0, 128, 256, 288, 320
Q0, D0, ROWS2 = 0, 128, 256


def dot_nt(a, b):
    return lax.dot_general(a, b, (((1,), (1,)), ((), ())), preferred_element_type=F32)


def dot_nn(a, b):
    return lax.dot_general(a, b, (((1,), (0,)), ((), ())), preferred_element_type=F32)


def kernel(
    heads_n,
    len_ref,
    mask_ref,
    q_hbm,
    k_hbm,
    v_hbm,
    mk_hbm,
    mv_hbm,
    w_hbm,
    og_hbm,
    lo_out,
    gw_out,
    gq_out,
    gk_out,
    gv_out,
    g1,
    g2,
    s_buf,
    w_buf,
    og_buf,
    ogx,
    do_scr,
    o_scr,
    on_scr,
    att_scr,
    ld,
    lo_own,
    lo_send,
    lo_recv,
    gs_send,
    gs_recv,
    gw_acc,
    gw_send,
    gw_recv,
    m_scr,
    l_scr,
    acc_scr,
    dq_scr,
    dk_scr,
    dv_scr,
    grads,
    lo_stage,
    gw_stage,
    local_sem,
    ring_ss,
    ring_rs,
    sib_ss,
    sib_rs,
    y_ss,
    y_rs,
    ld_ss,
    ld_rs,
    lo_ss,
    lo_rs,
    gw_ss,
    gw_rs,
    out_sem,
):
    ctx = lax.axis_index("ctx")
    head = lax.axis_index("head")
    core = lax.rem(ctx, 2)
    z = lax.rem(ctx // 2, NZ)
    i = ctx // (2 * NZ)
    scale = 1.0 / math.sqrt(HD)

    def at(ii, zz, cc):
        return {"ctx": (ii * NZ + zz) * 2 + cc}

    def z_at(off):
        return lax.rem(z + (off % NZ), NZ)

    y_dev = at(1 - i, z, core)
    sib_dev = at(i, z, 1 - core)
    own_cols = pl.ds(pl.multiple_of(i * HD, HD), HD)
    other_cols = pl.ds(pl.multiple_of((1 - i) * HD, HD), HD)
    gather = (g1, g2)
    started = []

    def remote(src, dst, ss, rs, dev):
        return pltpu.make_async_remote_copy(
            src_ref=src, dst_ref=dst, send_sem=ss, recv_sem=rs, device_id=dev, device_id_type=MESH
        )

    def go(copy):
        copy.start()
        started.append(copy)
        return copy

    piece = g1.at[0, 0, 0]
    local1 = [
        pltpu.make_async_copy(k_hbm.at[:, own_cols], piece.at[K0 : K0 + 128], local_sem.at[0]),
        pltpu.make_async_copy(v_hbm.at[:, own_cols], piece.at[V0 : V0 + 128], local_sem.at[1]),
        pltpu.make_async_copy(mk_hbm.at[:, own_cols], piece.at[MK0 : MK0 + 32], local_sem.at[2]),
        pltpu.make_async_copy(mv_hbm.at[:, own_cols], piece.at[MV0 : MV0 + 32], local_sem.at[3]),
    ]
    local_q = pltpu.make_async_copy(
        q_hbm.at[:, own_cols], g2.at[0, 0, 0, Q0 : Q0 + 128], local_sem.at[4]
    )
    local_w = pltpu.make_async_copy(w_hbm, w_buf, local_sem.at[5])
    local_og = pltpu.make_async_copy(og_hbm, og_buf, local_sem.at[6])
    for copy in local1:
        copy.start()
    local_q.start()
    local_og.start()
    local_w.start()

    barrier = pltpu.get_barrier_semaphore()
    peers = [y_dev, sib_dev]
    peers += [at(i, z_at(off), core) for off in range(1, NZ)]
    peers += [{"head": lax.rem(head + k, heads_n)} for k in range(1, heads_n)]
    for dev in peers:
        pl.semaphore_signal(barrier, inc=1, device_id=dev, device_id_type=MESH)
    pl.semaphore_wait(barrier, len(peers))

    far = g1.at[0, 0, 1]
    y_first = [
        remote(k_hbm.at[:, other_cols], far.at[K0 : K0 + 128], y_ss.at[0], y_rs.at[0], y_dev),
        remote(v_hbm.at[:, other_cols], far.at[V0 : V0 + 128], y_ss.at[1], y_rs.at[1], y_dev),
        remote(mk_hbm.at[:, other_cols], far.at[MK0 : MK0 + 32], y_ss.at[2], y_rs.at[2], y_dev),
        remote(mv_hbm.at[:, other_cols], far.at[MV0 : MV0 + 32], y_ss.at[3], y_rs.at[3], y_dev),
    ]
    y_q = remote(
        q_hbm.at[:, other_cols], g2.at[0, 0, 1, Q0 : Q0 + 128], y_ss.at[4], y_rs.at[4], y_dev
    )
    for copy in y_first:
        go(copy)
    go(y_q)

    def ring(phase, way, step, part):
        src = 0 if step == 0 else 2 * step - 1 + way
        dst = 7 if step == 3 else 2 * step + 1 + way
        buf = gather[phase]
        return remote(
            buf.at[0, src, part],
            buf.at[0, dst, part],
            ring_ss.at[phase, way, step, part],
            ring_rs.at[phase, way, step, part],
            at(i, z_at(1 if way == 0 else -1), core),
        )

    def ring_send(phase, step, part):
        for way in (0, 1):
            if step < 3 or part == way:
                go(ring(phase, way, step, part))

    def sib(phase, slot):
        buf = gather[phase]
        return remote(
            buf.at[0, slot], buf.at[1, slot], sib_ss.at[phase, slot], sib_rs.at[phase, slot], sib_dev
        )

    def advance(phase, step):
        if step < 3:
            for part in (0, 1):
                for way in (0, 1):
                    ring(phase, way, step, part).wait_recv()
                ring_send(phase, step + 1, part)
            go(sib(phase, 2 * step + 1))
            go(sib(phase, 2 * step + 2))
        else:
            ring(phase, 0, 3, 0).wait_recv()
            ring(phase, 1, 3, 1).wait_recv()
            go(sib(phase, 7))

    for copy in local1:
        copy.wait()
    ring_send(0, 0, 0)
    for copy in y_first:
        copy.wait_recv()
    ring_send(0, 0, 1)
    go(sib(0, 0))

    local_og.wait()
    local_w.wait()
    grad_att = dot_nt(og_buf[...], w_buf[...]).astype(BF16)
    do_scr[0] = grad_att[:, :HD]
    do_scr[1] = grad_att[:, HD:]
    g2[0, 0, 0, D0 : D0 + 128, :] = do_scr[i]
    y_do = go(
        remote(do_scr.at[1 - i], g2.at[0, 0, 1, D0 : D0 + 128], y_ss.at[5], y_rs.at[5], y_dev)
    )
    half = og_hbm.shape[1] // 2
    y_og = go(
        remote(
            og_hbm.at[:, pl.ds(pl.multiple_of((1 - i) * half, HD), half)],
            ogx,
            y_ss.at[6],
            y_rs.at[6],
            y_dev,
        )
    )
    local_q.wait()
    y_q.wait_recv()

    def block_of(part, slot, crel):
        ii = i if part == 0 else 1 - i
        cc = core if crel == 0 else 1 - core
        return (ii * NZ + z_at(OFFSET[slot])) * 2 + cc

    own_blocks = [block_of(0, 0, 0), block_of(1, 0, 0)]

    def both(buf, crel, slot, row, rows):
        return jnp.concatenate(
            [buf[crel, slot, 0, row : row + rows, :], buf[crel, slot, 1, row : row + rows, :]], axis=0
        )

    q_mine = both(g2, 0, 0, Q0, 128)
    m_scr[...] = jnp.full_like(m_scr, -jnp.inf)
    l_scr[...] = jnp.zeros_like(l_scr)
    acc_scr[...] = jnp.zeros_like(acc_scr)
    lane = lax.broadcasted_iota(jnp.int32, (1, 256), 1)

    def seq_scores(crel, slot):
        s = dot_nt(q_mine, both(g1, crel, slot, K0, 128)) * (scale * LOG2E)
        top = None
        for yq in (0, 1):
            row = []
            for yk in (0, 1):
                bias = jnp.where(
                    mask_ref[own_blocks[yq], block_of(yk, slot, crel)] > 0, 0.0, -jnp.inf
                )
                row.append(s[yq * 128 : yq * 128 + 128, yk * 128 : yk * 128 + 128] + bias)
                s_buf[crel * 8 + slot, yq * 128 : yq * 128 + 128, yk * 128 : yk * 128 + 128] = row[yk]
            both_k = jnp.maximum(row[0], row[1])
            top = both_k if top is None else jnp.concatenate([top, both_k], axis=0)
        return top

    def mem_rows(crel, group, row):
        return jnp.concatenate(
            [
                g1[crel, slot, part, row : row + 32, :]
                for slot in range(4 * group, 4 * group + 4)
                for part in (0, 1)
            ],
            axis=0,
        )

    def mem_scores(crel, group):
        s = dot_nt(q_mine, mem_rows(crel, group, MK0)) * (scale * LOG2E)
        base = jnp.zeros((1, 256), jnp.int32)
        place = 0
        for slot in range(4 * group, 4 * group + 4):
            for part in (0, 1):
                base = jnp.where(lane // 32 == place, block_of(part, slot, crel), base)
                place += 1
        index = base * 32 + lane % 32
        top = []
        for yq in (0, 1):
            allow = index < len_ref[own_blocks[yq]]
            t = jnp.where(allow, s[yq * 128 : yq * 128 + 128, :], -jnp.inf)
            s_buf[16 + crel * 2 + group, yq * 128 : yq * 128 + 128, :] = t
            top.append(jnp.maximum(t[:, :128], t[:, 128:]))
        return jnp.concatenate(top, axis=0)

    def absorb(chunks):
        tops = [mem_scores(*c[1:]) if c[0] else seq_scores(*c[1:]) for c in chunks]
        top = functools.reduce(jnp.maximum, tops)
        old = m_scr[...]
        new = jnp.maximum(old, jnp.broadcast_to(jnp.max(top, axis=1, keepdims=True), old.shape))
        fade = jnp.exp2(old - new)
        total = l_scr[...] * fade
        accum = acc_scr[...] * fade
        for mem, crel, slot in chunks:
            j = 16 + crel * 2 + slot if mem else crel * 8 + slot
            values = mem_rows(crel, slot, MV0) if mem else both(g1, crel, slot, V0, 128)
            p = jnp.exp2(s_buf[j] - jnp.concatenate([new, new], axis=1))
            total = total + p[:, :128] + p[:, 128:]
            high = p.astype(BF16)
            low = (p - high.astype(F32)).astype(BF16)
            accum = accum + dot_nn(high, values) + dot_nn(low, values)
        m_scr[...] = new
        l_scr[...] = total
        acc_scr[...] = accum

    def take_sib(phase, *slots):
        for slot in slots:
            sib(phase, slot).wait_recv()

    absorb([(0, 0, 0)])
    advance(0, 0)
    absorb([(0, 0, 1), (0, 0, 2)])
    take_sib(0, 0)
    absorb([(0, 1, 0)])
    advance(0, 1)
    absorb([(0, 0, 3), (0, 0, 4)])
    take_sib(0, 1, 2)
    absorb([(0, 1, 1), (0, 1, 2)])
    advance(0, 2)
    y_do.wait_recv()
    ring_send(1, 0, 0)
    ring_send(1, 0, 1)
    go(sib(1, 0))
    absorb([(0, 0, 5), (0, 0, 6), (1, 0, 0)])
    take_sib(0, 3, 4)
    absorb([(0, 1, 3), (0, 1, 4)])
    advance(0, 3)
    absorb([(0, 0, 7), (1, 0, 1)])
    take_sib(0, 5, 6)
    absorb([(0, 1, 5), (0, 1, 6), (1, 1, 0)])
    take_sib(0, 7)
    absorb([(0, 1, 7), (1, 1, 1)])

    total = jnp.broadcast_to(jnp.sum(l_scr[...], axis=1, keepdims=True), (256, 128))
    lse = m_scr[...] + jnp.log2(total)
    attended = (acc_scr[...] / total).astype(BF16)
    o_scr[...] = attended
    y_o = go(remote(o_scr, on_scr, y_ss.at[7], y_rs.at[7], y_dev))
    do_mine = both(g2, 0, 0, D0, 128)
    delta = jnp.broadcast_to(
        jnp.sum(do_mine.astype(F32) * attended.astype(F32), axis=1, keepdims=True), (256, 128)
    )
    m_scr[...] = lse
    l_scr[...] = delta
    eye = lax.broadcasted_iota(jnp.int32, (128, 128), 0) == lax.broadcasted_iota(
        jnp.int32, (128, 128), 1
    )
    ld[0, 0] = jnp.zeros((8, 256), F32)
    for yq in (0, 1):
        rows = slice(yq * 128, yq * 128 + 128)
        ld[0, 0, 0:1, rows] = jnp.sum(jnp.where(eye, lse[rows, :], 0.0), axis=0, keepdims=True)
        ld[0, 0, 1:2, rows] = jnp.sum(jnp.where(eye, delta[rows, :], 0.0), axis=0, keepdims=True)

    def ld_copy(off):
        slot = SLOT_OF[(-off) % NZ]
        return remote(
            ld.at[0, 0], ld.at[0, slot], ld_ss.at[slot - 1], ld_rs.at[slot - 1], at(i, z_at(off), core)
        )

    for off in (4, 3, 5, 2, 6, 1, 7):
        go(ld_copy(off))
    advance(1, 0)

    y_o.wait_recv()
    att_scr[i] = o_scr[0:128, :]
    att_scr[1 - i] = on_scr[128:256, :]
    att_own = jnp.concatenate([att_scr[0], att_scr[1]], axis=1)
    width = w_hbm.shape[1] // heads_n

    def lo_copy(k):
        return remote(
            lo_send.at[k - 1],
            lo_recv.at[k - 1],
            lo_ss.at[k - 1],
            lo_rs.at[k - 1],
            {"head": lax.rem(head + k, heads_n)},
        )

    for k in list(range(1, heads_n)) + [0]:
        cols = pl.ds(pl.multiple_of(lax.rem(head + k, heads_n) * width, HD), width)
        part = dot_nn(att_own, w_buf[:, cols])
        if k:
            lo_send[k - 1] = part.astype(BF16)
            go(lo_copy(k))
        else:
            lo_own[...] = part
    advance(1, 1)

    att_scr2 = jnp.concatenate([on_scr[128:256, :], on_scr[0:128, :]], axis=0)
    pair = (o_scr[...], att_scr2)
    att_t = jnp.concatenate(
        [
            jnp.where(i == 0, pair[0].astype(F32), pair[1].astype(F32)).T,
            jnp.where(i == 0, pair[1].astype(F32), pair[0].astype(F32)).T,
        ],
        axis=0,
    ).astype(BF16)
    y_og.wait_recv()

    def gw_part(k, cc):
        col = (z_at(k) * 2 + cc) * HD
        grads_in = jnp.concatenate(
            [
                og_buf[:, pl.ds(pl.multiple_of(i * half + col, HD), HD)],
                ogx[:, pl.ds(pl.multiple_of(col, HD), HD)],
            ],
            axis=0,
        )
        return dot_nn(att_t, grads_in)

    for k in range(NZ):
        gs_send[k] = gw_part(k, 1 - core).astype(BF16)
    gw_sib = go(remote(gs_send, gs_recv, y_ss.at[8], y_rs.at[8], sib_dev))
    for k in range(NZ):
        gw_acc[k] = gw_part(k, core)
    advance(1, 2)

    def gw_copy(k):
        return remote(
            gw_send.at[k - 1],
            gw_recv.at[k - 1],
            gw_ss.at[k - 1],
            gw_rs.at[k - 1],
            at(i, z_at(k), core),
        )

    gw_sib.wait_recv()
    for k in (4, 3, 5, 2, 6, 1, 7):
        gw_send[k - 1] = (gw_acc[k] + gs_recv[k].astype(F32)).astype(BF16)
        go(gw_copy(k))
    gw_own = gw_acc[0] + gs_recv[0].astype(F32)
    gw_acc[0] = gw_own

    for off in range(1, NZ):
        ld_copy(off).wait_recv()
    ld_sib = go(remote(ld.at[0], ld.at[1], y_ss.at[9], y_rs.at[9], sib_dev))

    dq_scr[...] = jnp.zeros_like(dq_scr)

    def query_step(j, keys, values):
        p = jnp.exp2(s_buf[j] - jnp.concatenate([m_scr[...], m_scr[...]], axis=1))
        dp = dot_nt(do_mine, values)
        ds = (p * (dp - jnp.concatenate([l_scr[...], l_scr[...]], axis=1))).astype(BF16)
        dq_scr[...] += dot_nn(ds, keys)

    def query_loop(slot, carry):
        for crel in (0, 1):
            query_step(
                crel * 8 + slot, both(g1, crel, slot, K0, 128), both(g1, crel, slot, V0, 128)
            )
        return carry

    lax.fori_loop(0, NZ, query_loop, 0)
    for crel in (0, 1):
        for group in (0, 1):
            query_step(
                16 + crel * 2 + group, mem_rows(crel, group, MK0), mem_rows(crel, group, MV0)
            )
    finish = []

    def give(kind, out, value):
        grads[kind] = value.astype(BF16)
        copy = pltpu.make_async_copy(grads.at[kind, 0:128], out.at[:, own_cols], out_sem.at[kind])
        copy.start()
        finish.append(copy)
        return go(
            remote(
                grads.at[kind, 128:256],
                out.at[:, own_cols],
                y_ss.at[10 + kind],
                y_rs.at[10 + kind],
                y_dev,
            )
        )

    given = [give(0, gq_out, dq_scr[...] * scale)]
    advance(1, 3)
    take_sib(1, *range(NZ))
    ld_sib.wait_recv()

    k_mine = both(g1, 0, 0, K0, 128)
    v_mine = both(g1, 0, 0, V0, 128)
    dk_scr[...] = jnp.zeros_like(dk_scr)
    dv_scr[...] = jnp.zeros_like(dv_scr)

    def key_step(crel, slot):
        queries = both(g2, crel, slot, Q0, 128)
        grad_out = both(g2, crel, slot, D0, 128)
        lse_row = ld[crel, slot, 0:1, :]
        delta_row = ld[crel, slot, 1:2, :]
        s = dot_nt(k_mine, queries) * (scale * LOG2E)
        rows = []
        for yk in (0, 1):
            row = []
            for yq in (0, 1):
                bias = jnp.where(
                    mask_ref[block_of(yq, slot, crel), own_blocks[yk]] > 0, 0.0, -jnp.inf
                )
                cut = slice(yq * 128, yq * 128 + 128)
                row.append(
                    jnp.exp2(s[yk * 128 : yk * 128 + 128, cut] + (bias - lse_row[:, cut]))
                )
            rows.append(jnp.concatenate(row, axis=1))
        p = jnp.concatenate(rows, axis=0)
        dp = dot_nt(v_mine, grad_out)
        ds = (p * (dp - delta_row)).astype(BF16)
        dv_scr[...] += dot_nn(p.astype(BF16), grad_out)
        dk_scr[...] += dot_nn(ds, queries)

    for slot in range(NZ):
        for crel in (0, 1):
            key_step(crel, slot)
    given.append(give(1, gk_out, dk_scr[...] * scale))
    given.append(give(2, gv_out, dv_scr[...]))

    result = lo_own[...]
    for k in range(1, heads_n):
        lo_copy(k).wait_recv()
        result = result + lo_recv[k - 1].astype(F32)
    lo_stage[...] = result.astype(BF16)
    copy = pltpu.make_async_copy(lo_stage, lo_out, out_sem.at[3])
    copy.start()
    finish.append(copy)
    result = gw_acc[0]
    for k in range(1, NZ):
        gw_copy(k).wait_recv()
        result = result + gw_recv[k - 1].astype(F32)
    gw_stage[...] = result.astype(BF16)
    copy = pltpu.make_async_copy(gw_stage, gw_out, out_sem.at[4])
    copy.start()
    finish.append(copy)

    for copy in given:
        copy.wait_recv()
    for copy in finish:
        copy.wait()
    for copy in started:
        copy.wait_send()


def per_device(
    queries,
    key_states,
    value_states,
    memory_keys,
    memory_values,
    memory_length,
    block_mask,
    out_weight,
    out_grad,
    *,
    heads_n,
):
    rows, cols = queries.shape
    d_model = out_weight.shape[1]
    width = d_model // heads_n
    hbm = pl.BlockSpec(memory_space=pltpu.HBM)
    smem = pl.BlockSpec(memory_space=pltpu.SMEM)
    vm = pltpu.VMEM
    dma = pltpu.SemaphoreType.DMA
    grad_shape = jax.ShapeDtypeStruct((rows, cols), BF16)
    return pl.pallas_call(
        functools.partial(kernel, heads_n),
        out_shape=(
            jax.ShapeDtypeStruct((rows, width), BF16),
            jax.ShapeDtypeStruct((cols, HD), BF16),
            grad_shape,
            grad_shape,
            grad_shape,
        ),
        in_specs=[smem, smem] + [hbm] * 7,
        out_specs=(hbm,) * 5,
        scratch_shapes=[
            vm((2, NZ, 2, ROWS1, HD), BF16),
            vm((2, NZ, 2, ROWS2, HD), BF16),
            vm((20, 256, 256), F32),
            vm((cols, d_model), BF16),
            vm((rows, d_model), BF16),
            vm((rows, d_model // 2), BF16),
            vm((2, rows, HD), BF16),
            vm((256, HD), BF16),
            vm((256, HD), BF16),
            vm((2, rows, HD), BF16),
            vm((2, NZ, 8, 256), F32),
            vm((rows, width), F32),
            vm((max(heads_n - 1, 1), rows, width), BF16),
            vm((max(heads_n - 1, 1), rows, width), BF16),
            vm((NZ, 256, HD), BF16),
            vm((NZ, 256, HD), BF16),
            vm((NZ, 256, HD), F32),
            vm((NZ - 1, 256, HD), BF16),
            vm((NZ - 1, 256, HD), BF16),
            vm((256, HD), F32),
            vm((256, HD), F32),
            vm((256, HD), F32),
            vm((256, HD), F32),
            vm((256, HD), F32),
            vm((256, HD), F32),
            vm((3, 256, HD), BF16),
            vm((rows, width), BF16),
            vm((cols, HD), BF16),
            dma((7,)),
            dma((2, 2, 4, 2)),
            dma((2, 2, 4, 2)),
            dma((2, NZ)),
            dma((2, NZ)),
            dma((13,)),
            dma((13,)),
            dma((NZ - 1,)),
            dma((NZ - 1,)),
            dma((max(heads_n - 1, 1),)),
            dma((max(heads_n - 1, 1),)),
            dma((NZ - 1,)),
            dma((NZ - 1,)),
            dma((5,)),
        ],
        compiler_params=pltpu.CompilerParams(
            collective_id=0, has_side_effects=True, vmem_limit_bytes=48 * 1024 * 1024
        ),
        name="attention",
    )(
        memory_length,
        block_mask,
        queries,
        key_states,
        value_states,
        memory_keys,
        memory_values,
        out_weight,
        out_grad,
    )


def solution(mesh):
    in_specs = (
        P("ctx", "head"),
        P("ctx", "head"),
        P("ctx", "head"),
        P("ctx", "head"),
        P("ctx", "head"),
        P(),
        P(),
        P("head", None),
        P("ctx", None),
    )
    out_specs = (
        P("ctx", "head"),
        P("head", "ctx"),
        P("ctx", "head"),
        P("ctx", "head"),
        P("ctx", "head"),
    )
    return jax.shard_map(
        functools.partial(per_device, heads_n=mesh.shape["head"]),
        mesh=mesh,
        in_specs=in_specs,
        out_specs=out_specs,
        check_vma=False,
    )
```

```python
import functools
import math

import jax
import jax.numpy as jnp
from jax import lax
from jax.experimental import pallas as pl
from jax.experimental.pallas import tpu as pltpu
from jax.sharding import PartitionSpec as P

HD = 128
BLK = 128
NZ = 8
NX = 4
LAG = 3
GW_ORDER = (4, 3, 5, 2, 6, 1, 7, 0)
F32 = jnp.float32
BF16 = jnp.bfloat16
MESH = pl.DeviceIdType.MESH
LOG2E = 1.4426950408889634

OFFSET = (0, -1, 1, -2, 2, -3, 3, 4)
SLOT_OF = {off % NZ: slot for slot, off in enumerate(OFFSET)}

K0, V0, MK0, MV0, ROWS1 = 0, 128, 256, 288, 320
Q0, D0, ROWS2 = 0, 128, 256


def dot_nt(a, b):
    return lax.dot_general(a, b, (((1,), (1,)), ((), ())), preferred_element_type=F32)


def dot_nn(a, b):
    return lax.dot_general(a, b, (((1,), (0,)), ((), ())), preferred_element_type=F32)


def kernel(
    heads_n,
    len_ref,
    mask_ref,
    q_hbm,
    k_hbm,
    v_hbm,
    mk_hbm,
    mv_hbm,
    w_hbm,
    og_hbm,
    lo_out,
    gw_out,
    gq_out,
    gk_out,
    gv_out,
    g1,
    g2,
    s_buf,
    w_buf,
    og_buf,
    ogx,
    do_scr,
    o_scr,
    on_scr,
    att_scr,
    ld,
    lo_own,
    lo_send,
    lo_recv,
    gs_send,
    gs_recv,
    gw_acc,
    gw_send,
    gw_recv,
    m_scr,
    l_scr,
    acc_scr,
    dq_scr,
    dk_scr,
    dv_scr,
    grads,
    lo_stage,
    gw_stage,
    local_sem,
    ring_ss,
    ring_rs,
    sib_ss,
    sib_rs,
    y_ss,
    y_rs,
    ld_ss,
    ld_rs,
    lo_ss,
    lo_rs,
    gw_ss,
    gw_rs,
    out_sem,
    hello,
):
    ctx = lax.axis_index("ctx")
    head = lax.axis_index("head")
    core = lax.rem(ctx, 2)
    z = lax.rem(ctx // 2, NZ)
    i = ctx // (2 * NZ)
    scale = 1.0 / math.sqrt(HD)

    def at(ii, zz, cc):
        return {"ctx": (ii * NZ + zz) * 2 + cc}

    def z_at(off):
        return lax.rem(z + (off % NZ), NZ)

    y_dev = at(1 - i, z, core)
    sib_dev = at(i, z, 1 - core)
    own_cols = pl.ds(pl.multiple_of(i * HD, HD), HD)
    other_cols = pl.ds(pl.multiple_of((1 - i) * HD, HD), HD)
    gather = (g1, g2)
    started = []

    def remote(src, dst, ss, rs, dev):
        return pltpu.make_async_remote_copy(
            src_ref=src, dst_ref=dst, send_sem=ss, recv_sem=rs, device_id=dev, device_id_type=MESH
        )

    def go(copy):
        copy.start()
        started.append(copy)
        return copy

    piece = g1.at[0, 0, 0]
    local1 = [
        pltpu.make_async_copy(k_hbm.at[:, own_cols], piece.at[K0 : K0 + 128], local_sem.at[0]),
        pltpu.make_async_copy(v_hbm.at[:, own_cols], piece.at[V0 : V0 + 128], local_sem.at[1]),
        pltpu.make_async_copy(mk_hbm.at[:, own_cols], piece.at[MK0 : MK0 + 32], local_sem.at[2]),
        pltpu.make_async_copy(mv_hbm.at[:, own_cols], piece.at[MV0 : MV0 + 32], local_sem.at[3]),
    ]
    local_q = pltpu.make_async_copy(
        q_hbm.at[:, own_cols], g2.at[0, 0, 0, Q0 : Q0 + 128], local_sem.at[4]
    )
    local_w = pltpu.make_async_copy(w_hbm, w_buf, local_sem.at[5])
    local_og = pltpu.make_async_copy(og_hbm, og_buf, local_sem.at[6])
    for copy in local1:
        copy.start()
    local_q.start()
    local_og.start()
    local_w.start()

    barrier = pltpu.get_barrier_semaphore()
    x = lax.rem(head, NX)
    row = head - x
    x_next = {"head": row + lax.rem(x + 1, NX)}
    x_last = {"head": row + lax.rem(x + NX - 1, NX)}
    row_dev = {"head": lax.rem(head + NX, heads_n)}
    peers = [y_dev, sib_dev, at(i, z_at(1), core), at(i, z_at(-1), core), x_next, x_last, row_dev]
    for dev in peers:
        pl.semaphore_signal(barrier, inc=1, device_id=dev, device_id_type=MESH)

    local_og.wait()
    local_w.wait()
    grad_att = dot_nt(og_buf[...], w_buf[...]).astype(BF16)
    do_scr[0] = grad_att[:, :HD]
    do_scr[1] = grad_att[:, HD:]
    g2[0, 0, 0, D0 : D0 + 128, :] = do_scr[i]
    pl.semaphore_wait(barrier, len(peers))

    far = g1.at[0, 0, 1]
    y_first = [
        remote(k_hbm.at[:, other_cols], far.at[K0 : K0 + 128], y_ss.at[0], y_rs.at[0], y_dev),
        remote(v_hbm.at[:, other_cols], far.at[V0 : V0 + 128], y_ss.at[1], y_rs.at[1], y_dev),
        remote(mk_hbm.at[:, other_cols], far.at[MK0 : MK0 + 32], y_ss.at[2], y_rs.at[2], y_dev),
        remote(mv_hbm.at[:, other_cols], far.at[MV0 : MV0 + 32], y_ss.at[3], y_rs.at[3], y_dev),
    ]
    y_q = remote(
        q_hbm.at[:, other_cols], g2.at[0, 0, 1, Q0 : Q0 + 128], y_ss.at[4], y_rs.at[4], y_dev
    )
    for copy in y_first:
        go(copy)
    go(y_q)
    y_do = go(
        remote(do_scr.at[1 - i], g2.at[0, 0, 1, D0 : D0 + 128], y_ss.at[5], y_rs.at[5], y_dev)
    )

    def ring(phase, way, step, part):
        src = 0 if step == 0 else 2 * step - 1 + way
        dst = 7 if step == 3 else 2 * step + 1 + way
        buf = gather[phase]
        return remote(
            buf.at[0, src, part],
            buf.at[0, dst, part],
            ring_ss.at[phase, way, step, part],
            ring_rs.at[phase, way, step, part],
            at(i, z_at(1 if way == 0 else -1), core),
        )

    def ring_send(phase, step, part):
        for way in (0, 1):
            if step < 3 or part == way:
                go(ring(phase, way, step, part))

    def sib(phase, slot):
        buf = gather[phase]
        return remote(
            buf.at[0, slot], buf.at[1, slot], sib_ss.at[phase, slot], sib_rs.at[phase, slot], sib_dev
        )

    def follow(step):
        if step == LAG - 1:
            if LAG == 0:
                local_q.wait()
            ring_send(1, 0, 0)
            if LAG == 0:
                y_q.wait_recv()
            y_do.wait_recv()
            ring_send(1, 0, 1)
            go(sib(1, 0))
        elif step >= LAG:
            advance(1, step - LAG)

    def take(phase, step, part):
        for way in (0, 1):
            ring(phase, way, step, part).wait_recv()
            if step < 2 or part == way:
                go(ring(phase, way, step + 1, part))

    def advance(phase, step):
        if step < 3:
            for part in (0, 1):
                if (phase, step, part) != (0, 0, 0):
                    take(phase, step, part)
            go(sib(phase, 2 * step + 1))
            go(sib(phase, 2 * step + 2))
        else:
            ring(phase, 0, 3, 0).wait_recv()
            ring(phase, 1, 3, 1).wait_recv()
            go(sib(phase, 7))

    for copy in local1:
        copy.wait()
    ring_send(0, 0, 0)
    pl.semaphore_signal(hello.at[0], inc=1, device_id=x_next, device_id_type=MESH)

    take(0, 0, 0)
    for copy in y_first:
        copy.wait_recv()
    ring_send(0, 0, 1)
    go(sib(0, 0))
    half = og_hbm.shape[1] // 2
    y_og = go(
        remote(
            og_hbm.at[:, pl.ds(pl.multiple_of((1 - i) * half, HD), half)],
            ogx,
            y_ss.at[6],
            y_rs.at[6],
            y_dev,
        )
    )
    follow(-1)
    if LAG > 0:
        local_q.wait()
        y_q.wait_recv()

    def block_of(part, slot, crel):
        ii = i if part == 0 else 1 - i
        cc = core if crel == 0 else 1 - core
        return (ii * NZ + z_at(OFFSET[slot])) * 2 + cc

    own_blocks = [block_of(0, 0, 0), block_of(1, 0, 0)]

    def both(buf, crel, slot, row, rows):
        return jnp.concatenate(
            [buf[crel, slot, 0, row : row + rows, :], buf[crel, slot, 1, row : row + rows, :]], axis=0
        )

    q_mine = both(g2, 0, 0, Q0, 128)
    m_scr[...] = jnp.full_like(m_scr, -jnp.inf)
    l_scr[...] = jnp.zeros_like(l_scr)
    acc_scr[...] = jnp.zeros_like(acc_scr)
    lane = lax.broadcasted_iota(jnp.int32, (1, 256), 1)

    def seq_scores(crel, slot):
        s = dot_nt(q_mine, both(g1, crel, slot, K0, 128)) * (scale * LOG2E)
        top = None
        for yq in (0, 1):
            row = []
            for yk in (0, 1):
                bias = jnp.where(
                    mask_ref[own_blocks[yq], block_of(yk, slot, crel)] > 0, 0.0, -jnp.inf
                )
                row.append(s[yq * 128 : yq * 128 + 128, yk * 128 : yk * 128 + 128] + bias)
                s_buf[crel * 8 + slot, yq * 128 : yq * 128 + 128, yk * 128 : yk * 128 + 128] = row[yk]
            both_k = jnp.maximum(row[0], row[1])
            top = both_k if top is None else jnp.concatenate([top, both_k], axis=0)
        return top

    def mem_rows(crel, group, row):
        return jnp.concatenate(
            [
                g1[crel, slot, part, row : row + 32, :]
                for slot in range(4 * group, 4 * group + 4)
                for part in (0, 1)
            ],
            axis=0,
        )

    def mem_scores(crel, group):
        s = dot_nt(q_mine, mem_rows(crel, group, MK0)) * (scale * LOG2E)
        base = jnp.zeros((1, 256), jnp.int32)
        place = 0
        for slot in range(4 * group, 4 * group + 4):
            for part in (0, 1):
                base = jnp.where(lane // 32 == place, block_of(part, slot, crel), base)
                place += 1
        index = base * 32 + lane % 32
        top = []
        for yq in (0, 1):
            allow = index < len_ref[own_blocks[yq]]
            t = jnp.where(allow, s[yq * 128 : yq * 128 + 128, :], -jnp.inf)
            s_buf[16 + crel * 2 + group, yq * 128 : yq * 128 + 128, :] = t
            top.append(jnp.maximum(t[:, :128], t[:, 128:]))
        return jnp.concatenate(top, axis=0)

    def absorb(chunks):
        tops = [mem_scores(*c[1:]) if c[0] else seq_scores(*c[1:]) for c in chunks]
        top = functools.reduce(jnp.maximum, tops)
        old = m_scr[...]
        new = jnp.maximum(old, jnp.broadcast_to(jnp.max(top, axis=1, keepdims=True), old.shape))
        fade = jnp.exp2(old - new)
        total = l_scr[...] * fade
        accum = acc_scr[...] * fade
        for mem, crel, slot in chunks:
            j = 16 + crel * 2 + slot if mem else crel * 8 + slot
            values = mem_rows(crel, slot, MV0) if mem else both(g1, crel, slot, V0, 128)
            p = jnp.exp2(s_buf[j] - jnp.concatenate([new, new], axis=1))
            total = total + p[:, :128] + p[:, 128:]
            high = p.astype(BF16)
            low = (p - high.astype(F32)).astype(BF16)
            accum = accum + dot_nn(high, values) + dot_nn(low, values)
        m_scr[...] = new
        l_scr[...] = total
        acc_scr[...] = accum

    def late(step):
        if step > 3 - LAG:
            advance(1, step)

    def take_sib(phase, *slots):
        for slot in slots:
            sib(phase, slot).wait_recv()

    absorb([(0, 0, 0)])
    pl.semaphore_wait(hello.at[0], 1)
    pl.semaphore_signal(hello.at[1], inc=1, device_id=row_dev, device_id_type=MESH)
    advance(0, 0)
    follow(0)
    absorb([(0, 0, 1), (0, 0, 2)])
    take_sib(0, 0)
    absorb([(0, 1, 0)])
    advance(0, 1)
    follow(1)
    absorb([(0, 0, 3), (0, 0, 4)])
    take_sib(0, 1, 2)
    absorb([(0, 1, 1), (0, 1, 2)])
    advance(0, 2)
    follow(2)
    absorb([(0, 0, 5), (0, 0, 6), (1, 0, 0)])
    take_sib(0, 3, 4)
    absorb([(0, 1, 3), (0, 1, 4)])
    advance(0, 3)
    follow(3)
    absorb([(0, 0, 7), (1, 0, 1)])
    take_sib(0, 5, 6)
    absorb([(0, 1, 5), (0, 1, 6), (1, 1, 0)])
    take_sib(0, 7)
    absorb([(0, 1, 7), (1, 1, 1)])

    total = jnp.broadcast_to(jnp.sum(l_scr[...], axis=1, keepdims=True), (256, 128))
    lse = m_scr[...] + jnp.log2(total)
    attended = (acc_scr[...] / total).astype(BF16)
    o_scr[...] = attended
    y_o = go(remote(o_scr, on_scr, y_ss.at[7], y_rs.at[7], y_dev))
    do_mine = both(g2, 0, 0, D0, 128)
    delta = jnp.broadcast_to(
        jnp.sum(do_mine.astype(F32) * attended.astype(F32), axis=1, keepdims=True), (256, 128)
    )
    m_scr[...] = lse
    l_scr[...] = delta
    eye = lax.broadcasted_iota(jnp.int32, (128, 128), 0) == lax.broadcasted_iota(
        jnp.int32, (128, 128), 1
    )
    ld[0, 0] = jnp.zeros((8, 256), F32)
    for yq in (0, 1):
        rows = slice(yq * 128, yq * 128 + 128)
        ld[0, 0, 0:1, rows] = jnp.sum(jnp.where(eye, lse[rows, :], 0.0), axis=0, keepdims=True)
        ld[0, 0, 1:2, rows] = jnp.sum(jnp.where(eye, delta[rows, :], 0.0), axis=0, keepdims=True)

    def ld_copy(off):
        slot = SLOT_OF[(-off) % NZ]
        return remote(
            ld.at[0, 0], ld.at[0, slot], ld_ss.at[slot - 1], ld_rs.at[slot - 1], at(i, z_at(off), core)
        )

    for off in (4, 3, 5, 2, 6, 1, 7):
        go(ld_copy(off))
    late(0)

    dq_scr[...] = jnp.zeros_like(dq_scr)

    def query_step(j, keys, values):
        p = jnp.exp2(s_buf[j] - jnp.concatenate([m_scr[...], m_scr[...]], axis=1))
        dp = dot_nt(do_mine, values)
        ds = (p * (dp - jnp.concatenate([l_scr[...], l_scr[...]], axis=1))).astype(BF16)
        dq_scr[...] += dot_nn(ds, keys)

    def query_loop(slot, carry):
        for crel in (0, 1):
            query_step(
                crel * 8 + slot, both(g1, crel, slot, K0, 128), both(g1, crel, slot, V0, 128)
            )
        return carry

    lax.fori_loop(0, 3, query_loop, 0)
    late(1)
    lax.fori_loop(3, 5, query_loop, 0)

    y_o.wait_recv()
    att_scr2 = jnp.concatenate([on_scr[128:256, :], on_scr[0:128, :]], axis=0)
    pair = (o_scr[...], att_scr2)
    att_t = jnp.concatenate(
        [
            jnp.where(i == 0, pair[0].astype(F32), pair[1].astype(F32)).T,
            jnp.where(i == 0, pair[1].astype(F32), pair[0].astype(F32)).T,
        ],
        axis=0,
    ).astype(BF16)
    y_og.wait_recv()

    def gw_part(k, cc):
        col = (z_at(k) * 2 + cc) * HD
        grads_in = jnp.concatenate(
            [
                og_buf[:, pl.ds(pl.multiple_of(i * half + col, HD), HD)],
                ogx[:, pl.ds(pl.multiple_of(col, HD), HD)],
            ],
            axis=0,
        )
        return dot_nn(att_t, grads_in)

    gw_sib = []
    for place, k in enumerate(GW_ORDER):
        gs_send[place] = gw_part(k, 1 - core).astype(BF16)
        if place % 4 == 3:
            cut = slice(place - 3, place + 1)
            n = 8 if place == 3 else 13
            gw_sib.append(
                go(remote(gs_send.at[cut], gs_recv.at[cut], y_ss.at[n], y_rs.at[n], sib_dev))
            )
    for place, k in enumerate(GW_ORDER):
        gw_acc[place] = gw_part(k, core)
    late(2)

    def gw_copy(k):
        return remote(
            gw_send.at[k - 1],
            gw_recv.at[k - 1],
            gw_ss.at[k - 1],
            gw_rs.at[k - 1],
            at(i, z_at(k), core),
        )

    for place, k in enumerate(GW_ORDER):
        if place % 4 == 0:
            gw_sib[place // 4].wait_recv()
        block = gw_acc[place] + gs_recv[place].astype(F32)
        if k:
            gw_send[k - 1] = block.astype(BF16)
            go(gw_copy(k))
        else:
            gw_acc[0] = block

    pl.semaphore_wait(hello.at[1], 1)
    att_scr[i] = o_scr[0:128, :]
    att_scr[1 - i] = on_scr[128:256, :]
    att_own = jnp.concatenate([att_scr[0], att_scr[1]], axis=1)
    width = w_hbm.shape[1] // heads_n

    def lo_copy(k):
        return remote(
            lo_send.at[k - 1],
            lo_recv.at[k - 1],
            lo_ss.at[k - 1],
            lo_rs.at[k - 1],
            {"head": lax.rem(head + k, heads_n)},
        )

    for k in list(range(1, heads_n)) + [0]:
        cols = pl.ds(pl.multiple_of(lax.rem(head + k, heads_n) * width, HD), width)
        part = dot_nn(att_own, w_buf[:, cols])
        if k:
            lo_send[k - 1] = part.astype(BF16)
            go(lo_copy(k))
        else:
            lo_own[...] = part

    for off in range(1, NZ):
        ld_copy(off).wait_recv()
    ld_sib = go(remote(ld.at[0], ld.at[1], y_ss.at[9], y_rs.at[9], sib_dev))
    lax.fori_loop(5, NZ, query_loop, 0)
    for crel in (0, 1):
        for group in (0, 1):
            query_step(
                16 + crel * 2 + group, mem_rows(crel, group, MK0), mem_rows(crel, group, MV0)
            )
    finish = []

    def give(kind, out, value):
        grads[kind] = value.astype(BF16)
        copy = pltpu.make_async_copy(grads.at[kind, 0:128], out.at[:, own_cols], out_sem.at[kind])
        copy.start()
        finish.append(copy)
        return go(
            remote(
                grads.at[kind, 128:256],
                out.at[:, own_cols],
                y_ss.at[10 + kind],
                y_rs.at[10 + kind],
                y_dev,
            )
        )

    given = [give(0, gq_out, dq_scr[...] * scale)]
    late(3)
    take_sib(1, *range(NZ))
    ld_sib.wait_recv()

    k_mine = both(g1, 0, 0, K0, 128)
    v_mine = both(g1, 0, 0, V0, 128)
    dk_scr[...] = jnp.zeros_like(dk_scr)
    dv_scr[...] = jnp.zeros_like(dv_scr)

    def key_step(crel, slot):
        queries = both(g2, crel, slot, Q0, 128)
        grad_out = both(g2, crel, slot, D0, 128)
        lse_row = ld[crel, slot, 0:1, :]
        delta_row = ld[crel, slot, 1:2, :]
        s = dot_nt(k_mine, queries) * (scale * LOG2E)
        rows = []
        for yk in (0, 1):
            row = []
            for yq in (0, 1):
                bias = jnp.where(
                    mask_ref[block_of(yq, slot, crel), own_blocks[yk]] > 0, 0.0, -jnp.inf
                )
                cut = slice(yq * 128, yq * 128 + 128)
                row.append(
                    jnp.exp2(s[yk * 128 : yk * 128 + 128, cut] + (bias - lse_row[:, cut]))
                )
            rows.append(jnp.concatenate(row, axis=1))
        p = jnp.concatenate(rows, axis=0)
        dp = dot_nt(v_mine, grad_out)
        ds = (p * (dp - delta_row)).astype(BF16)
        dv_scr[...] += dot_nn(p.astype(BF16), grad_out)
        dk_scr[...] += dot_nn(ds, queries)

    for slot in range(NZ):
        for crel in (0, 1):
            key_step(crel, slot)
    given.append(give(1, gk_out, dk_scr[...] * scale))
    given.append(give(2, gv_out, dv_scr[...]))

    result = lo_own[...]
    for k in range(1, heads_n):
        lo_copy(k).wait_recv()
        result = result + lo_recv[k - 1].astype(F32)
    lo_stage[...] = result.astype(BF16)
    copy = pltpu.make_async_copy(lo_stage, lo_out, out_sem.at[3])
    copy.start()
    finish.append(copy)
    result = gw_acc[0]
    for k in range(1, NZ):
        gw_copy(k).wait_recv()
        result = result + gw_recv[k - 1].astype(F32)
    gw_stage[...] = result.astype(BF16)
    copy = pltpu.make_async_copy(gw_stage, gw_out, out_sem.at[4])
    copy.start()
    finish.append(copy)

    for copy in given:
        copy.wait_recv()
    for copy in finish:
        copy.wait()
    for copy in started:
        copy.wait_send()


def hand_out(*refs):
    ins, outs, held, sems = refs[:5], refs[5:10], refs[10:15], refs[15]
    reads = [pltpu.make_async_copy(ins[n], held[n], sems.at[0, n]) for n in range(5)]
    writes = [pltpu.make_async_copy(held[n], outs[n], sems.at[1, n]) for n in range(5)]
    for copy in reads:
        copy.start()
    for n in range(5):
        reads[n].wait()
        writes[n].start()
    for copy in writes:
        copy.wait()


def per_device(
    queries,
    key_states,
    value_states,
    memory_keys,
    memory_values,
    memory_length,
    block_mask,
    out_weight,
    out_grad,
    *,
    heads_n,
):
    rows, cols = queries.shape
    d_model = out_weight.shape[1]
    width = d_model // heads_n
    hbm = pl.BlockSpec(memory_space=pltpu.HBM)
    smem = pl.BlockSpec(memory_space=pltpu.SMEM)
    vm = pltpu.VMEM
    dma = pltpu.SemaphoreType.DMA
    grad_shape = jax.ShapeDtypeStruct((rows, cols), BF16)
    results = pl.pallas_call(
        functools.partial(kernel, heads_n),
        out_shape=(
            jax.ShapeDtypeStruct((rows, width), BF16),
            jax.ShapeDtypeStruct((cols, HD), BF16),
            grad_shape,
            grad_shape,
            grad_shape,
        ),
        in_specs=[smem, smem] + [hbm] * 7,
        out_specs=(hbm,) * 5,
        scratch_shapes=[
            vm((2, NZ, 2, ROWS1, HD), BF16),
            vm((2, NZ, 2, ROWS2, HD), BF16),
            vm((20, 256, 256), F32),
            vm((cols, d_model), BF16),
            vm((rows, d_model), BF16),
            vm((rows, d_model // 2), BF16),
            vm((2, rows, HD), BF16),
            vm((256, HD), BF16),
            vm((256, HD), BF16),
            vm((2, rows, HD), BF16),
            vm((2, NZ, 8, 256), F32),
            vm((rows, width), F32),
            vm((max(heads_n - 1, 1), rows, width), BF16),
            vm((max(heads_n - 1, 1), rows, width), BF16),
            vm((NZ, 256, HD), BF16),
            vm((NZ, 256, HD), BF16),
            vm((NZ, 256, HD), F32),
            vm((NZ - 1, 256, HD), BF16),
            vm((NZ - 1, 256, HD), BF16),
            vm((256, HD), F32),
            vm((256, HD), F32),
            vm((256, HD), F32),
            vm((256, HD), F32),
            vm((256, HD), F32),
            vm((256, HD), F32),
            vm((3, 256, HD), BF16),
            vm((rows, width), BF16),
            vm((cols, HD), BF16),
            dma((7,)),
            dma((2, 2, 4, 2)),
            dma((2, 2, 4, 2)),
            dma((2, NZ)),
            dma((2, NZ)),
            dma((14,)),
            dma((14,)),
            dma((NZ - 1,)),
            dma((NZ - 1,)),
            dma((max(heads_n - 1, 1),)),
            dma((max(heads_n - 1, 1),)),
            dma((NZ - 1,)),
            dma((NZ - 1,)),
            dma((5,)),
            pltpu.SemaphoreType.REGULAR((2,)),
        ],
        compiler_params=pltpu.CompilerParams(
            collective_id=0, has_side_effects=True, vmem_limit_bytes=56 * 1024 * 1024
        ),
        name="attention",
    )(
        memory_length,
        block_mask,
        queries,
        key_states,
        value_states,
        memory_keys,
        memory_values,
        out_weight,
        out_grad,
    )
    return pl.pallas_call(
        hand_out,
        out_shape=tuple(jax.ShapeDtypeStruct(r.shape, r.dtype) for r in results),
        in_specs=[hbm] * 5,
        out_specs=(hbm,) * 5,
        scratch_shapes=[vm(r.shape, r.dtype) for r in results] + [dma((2, 5))],
        name="results",
    )(*results)


def solution(mesh):
    in_specs = (
        P("ctx", "head"),
        P("ctx", "head"),
        P("ctx", "head"),
        P("ctx", "head"),
        P("ctx", "head"),
        P(),
        P(),
        P("head", None),
        P("ctx", None),
    )
    out_specs = (
        P("ctx", "head"),
        P("head", "ctx"),
        P("ctx", "head"),
        P("ctx", "head"),
        P("ctx", "head"),
    )
    return jax.shard_map(
        functools.partial(per_device, heads_n=mesh.shape["head"]),
        mesh=mesh,
        in_specs=in_specs,
        out_specs=out_specs,
        check_vma=False,
    )
```

```python
import functools
import math

import jax
import jax.numpy as jnp
from jax import lax
from jax.experimental import pallas as pl
from jax.experimental.pallas import tpu as pltpu
from jax.sharding import PartitionSpec as P

HD = 128
BLK = 128
NZ = 8
NX = 4
LAG = 3
GW_ORDER = (4, 3, 5, 2, 6, 1, 7, 0)
F32 = jnp.float32
BF16 = jnp.bfloat16
MESH = pl.DeviceIdType.MESH
LOG2E = 1.4426950408889634

OFFSET = (0, -1, 1, -2, 2, -3, 3, 4)
SLOT_OF = {off % NZ: slot for slot, off in enumerate(OFFSET)}

K0, V0, MK0, MV0, ROWS1 = 0, 128, 256, 288, 320
Q0, D0, ROWS2 = 0, 128, 256


def dot_nt(a, b):
    return lax.dot_general(a, b, (((1,), (1,)), ((), ())), preferred_element_type=F32)


def dot_nn(a, b):
    return lax.dot_general(a, b, (((1,), (0,)), ((), ())), preferred_element_type=F32)


def kernel(
    heads_n,
    len_ref,
    mask_ref,
    q_hbm,
    k_hbm,
    v_hbm,
    mk_hbm,
    mv_hbm,
    w_hbm,
    og_hbm,
    lo_out,
    gw_out,
    gq_out,
    gk_out,
    gv_out,
    g1,
    g2,
    s_buf,
    w_buf,
    og_buf,
    ogx,
    do_scr,
    o_scr,
    on_scr,
    att_scr,
    ld,
    lo_own,
    lo_send,
    lo_recv,
    gs_send,
    gs_recv,
    gw_acc,
    gw_send,
    gw_recv,
    m_scr,
    l_scr,
    acc_scr,
    dq_scr,
    dk_scr,
    dv_scr,
    grads,
    lo_stage,
    gw_stage,
    local_sem,
    ring_ss,
    ring_rs,
    sib_ss,
    sib_rs,
    y_ss,
    y_rs,
    ld_ss,
    ld_rs,
    lo_ss,
    lo_rs,
    gw_ss,
    gw_rs,
    out_sem,
    hello,
):
    ctx = lax.axis_index("ctx")
    head = lax.axis_index("head")
    core = lax.rem(ctx, 2)
    z = lax.rem(ctx // 2, NZ)
    i = ctx // (2 * NZ)
    scale = 1.0 / math.sqrt(HD)

    def at(ii, zz, cc):
        return {"ctx": (ii * NZ + zz) * 2 + cc}

    def z_at(off):
        return lax.rem(z + (off % NZ), NZ)

    y_dev = at(1 - i, z, core)
    sib_dev = at(i, z, 1 - core)
    own_cols = pl.ds(pl.multiple_of(i * HD, HD), HD)
    other_cols = pl.ds(pl.multiple_of((1 - i) * HD, HD), HD)
    gather = (g1, g2)
    started = []

    def remote(src, dst, ss, rs, dev):
        return pltpu.make_async_remote_copy(
            src_ref=src, dst_ref=dst, send_sem=ss, recv_sem=rs, device_id=dev, device_id_type=MESH
        )

    def go(copy):
        copy.start()
        started.append(copy)
        return copy

    piece = g1.at[0, 0, 0]
    local1 = [
        pltpu.make_async_copy(k_hbm.at[:, own_cols], piece.at[K0 : K0 + 128], local_sem.at[0]),
        pltpu.make_async_copy(v_hbm.at[:, own_cols], piece.at[V0 : V0 + 128], local_sem.at[1]),
        pltpu.make_async_copy(mk_hbm.at[:, own_cols], piece.at[MK0 : MK0 + 32], local_sem.at[2]),
        pltpu.make_async_copy(mv_hbm.at[:, own_cols], piece.at[MV0 : MV0 + 32], local_sem.at[3]),
    ]
    local_q = pltpu.make_async_copy(
        q_hbm.at[:, own_cols], g2.at[0, 0, 0, Q0 : Q0 + 128], local_sem.at[4]
    )
    local_w = pltpu.make_async_copy(w_hbm, w_buf, local_sem.at[5])
    local_og = pltpu.make_async_copy(og_hbm, og_buf, local_sem.at[6])
    for copy in local1:
        copy.start()
    local_q.start()
    local_og.start()
    local_w.start()

    barrier = pltpu.get_barrier_semaphore()
    x = lax.rem(head, NX)
    row = head - x
    x_next = {"head": row + lax.rem(x + 1, NX)}
    x_last = {"head": row + lax.rem(x + NX - 1, NX)}
    row_dev = {"head": lax.rem(head + NX, heads_n)}
    peers = [y_dev, sib_dev, at(i, z_at(1), core), at(i, z_at(-1), core), x_next, x_last, row_dev]
    for dev in peers:
        pl.semaphore_signal(barrier, inc=1, device_id=dev, device_id_type=MESH)

    local_og.wait()
    local_w.wait()
    grad_att = dot_nt(og_buf[...], w_buf[...]).astype(BF16)
    do_scr[0] = grad_att[:, :HD]
    do_scr[1] = grad_att[:, HD:]
    g2[0, 0, 0, D0 : D0 + 128, :] = do_scr[i]
    pl.semaphore_wait(barrier, len(peers))

    far = g1.at[0, 0, 1]
    y_first = [
        remote(k_hbm.at[:, other_cols], far.at[K0 : K0 + 128], y_ss.at[0], y_rs.at[0], y_dev),
        remote(v_hbm.at[:, other_cols], far.at[V0 : V0 + 128], y_ss.at[1], y_rs.at[1], y_dev),
        remote(mk_hbm.at[:, other_cols], far.at[MK0 : MK0 + 32], y_ss.at[2], y_rs.at[2], y_dev),
        remote(mv_hbm.at[:, other_cols], far.at[MV0 : MV0 + 32], y_ss.at[3], y_rs.at[3], y_dev),
    ]
    y_q = remote(
        q_hbm.at[:, other_cols], g2.at[0, 0, 1, Q0 : Q0 + 128], y_ss.at[4], y_rs.at[4], y_dev
    )
    for copy in y_first:
        go(copy)
    go(y_q)
    y_do = go(
        remote(do_scr.at[1 - i], g2.at[0, 0, 1, D0 : D0 + 128], y_ss.at[5], y_rs.at[5], y_dev)
    )

    def ring(phase, way, step, part):
        src = 0 if step == 0 else 2 * step - 1 + way
        dst = 7 if step == 3 else 2 * step + 1 + way
        buf = gather[phase]
        return remote(
            buf.at[0, src, part],
            buf.at[0, dst, part],
            ring_ss.at[phase, way, step, part],
            ring_rs.at[phase, way, step, part],
            at(i, z_at(1 if way == 0 else -1), core),
        )

    def ring_send(phase, step, part):
        for way in (0, 1):
            if step < 3 or part == way:
                go(ring(phase, way, step, part))

    def sib(phase, slot):
        buf = gather[phase]
        return remote(
            buf.at[0, slot], buf.at[1, slot], sib_ss.at[phase, slot], sib_rs.at[phase, slot], sib_dev
        )

    def follow(step):
        if step == LAG - 1:
            if LAG == 0:
                local_q.wait()
            ring_send(1, 0, 0)
            if LAG == 0:
                y_q.wait_recv()
            y_do.wait_recv()
            ring_send(1, 0, 1)
            go(sib(1, 0))
        elif step >= LAG:
            advance(1, step - LAG)

    def take(phase, step, part):
        for way in (0, 1):
            ring(phase, way, step, part).wait_recv()
            if step < 2 or part == way:
                go(ring(phase, way, step + 1, part))

    def advance(phase, step):
        if step < 3:
            for part in (0, 1):
                if (phase, step, part) != (0, 0, 0):
                    take(phase, step, part)
            go(sib(phase, 2 * step + 1))
            go(sib(phase, 2 * step + 2))
        else:
            ring(phase, 0, 3, 0).wait_recv()
            ring(phase, 1, 3, 1).wait_recv()
            go(sib(phase, 7))

    for copy in local1:
        copy.wait()
    ring_send(0, 0, 0)
    pl.semaphore_signal(hello.at[0], inc=1, device_id=x_next, device_id_type=MESH)

    take(0, 0, 0)
    for copy in y_first:
        copy.wait_recv()
    ring_send(0, 0, 1)
    go(sib(0, 0))
    half = og_hbm.shape[1] // 2
    y_og = go(
        remote(
            og_hbm.at[:, pl.ds(pl.multiple_of((1 - i) * half, HD), half)],
            ogx,
            y_ss.at[6],
            y_rs.at[6],
            y_dev,
        )
    )
    follow(-1)
    if LAG > 0:
        local_q.wait()
        y_q.wait_recv()

    def block_of(part, slot, crel):
        ii = i if part == 0 else 1 - i
        cc = core if crel == 0 else 1 - core
        return (ii * NZ + z_at(OFFSET[slot])) * 2 + cc

    own_blocks = [block_of(0, 0, 0), block_of(1, 0, 0)]

    def both(buf, crel, slot, row, rows):
        return jnp.concatenate(
            [buf[crel, slot, 0, row : row + rows, :], buf[crel, slot, 1, row : row + rows, :]], axis=0
        )

    q_mine = both(g2, 0, 0, Q0, 128)
    m_scr[...] = jnp.full_like(m_scr, -jnp.inf)
    l_scr[...] = jnp.zeros_like(l_scr)
    acc_scr[...] = jnp.zeros_like(acc_scr)
    lane = lax.broadcasted_iota(jnp.int32, (1, 256), 1)

    def seq_scores(crel, slot):
        s = dot_nt(q_mine, both(g1, crel, slot, K0, 128)) * (scale * LOG2E)
        top = None
        for yq in (0, 1):
            row = []
            for yk in (0, 1):
                bias = jnp.where(
                    mask_ref[own_blocks[yq], block_of(yk, slot, crel)] > 0, 0.0, -jnp.inf
                )
                row.append(s[yq * 128 : yq * 128 + 128, yk * 128 : yk * 128 + 128] + bias)
                s_buf[crel * 8 + slot, yq * 128 : yq * 128 + 128, yk * 128 : yk * 128 + 128] = row[yk]
            both_k = jnp.maximum(row[0], row[1])
            top = both_k if top is None else jnp.concatenate([top, both_k], axis=0)
        return top

    def mem_rows(crel, group, row):
        return jnp.concatenate(
            [
                g1[crel, slot, part, row : row + 32, :]
                for slot in range(4 * group, 4 * group + 4)
                for part in (0, 1)
            ],
            axis=0,
        )

    def mem_scores(crel, group):
        s = dot_nt(q_mine, mem_rows(crel, group, MK0)) * (scale * LOG2E)
        base = jnp.zeros((1, 256), jnp.int32)
        place = 0
        for slot in range(4 * group, 4 * group + 4):
            for part in (0, 1):
                base = jnp.where(lane // 32 == place, block_of(part, slot, crel), base)
                place += 1
        index = base * 32 + lane % 32
        top = []
        for yq in (0, 1):
            allow = index < len_ref[own_blocks[yq]]
            t = jnp.where(allow, s[yq * 128 : yq * 128 + 128, :], -jnp.inf)
            s_buf[16 + crel * 2 + group, yq * 128 : yq * 128 + 128, :] = t
            top.append(jnp.maximum(t[:, :128], t[:, 128:]))
        return jnp.concatenate(top, axis=0)

    def absorb(chunks):
        tops = [mem_scores(*c[1:]) if c[0] else seq_scores(*c[1:]) for c in chunks]
        top = functools.reduce(jnp.maximum, tops)
        old = m_scr[...]
        new = jnp.maximum(old, jnp.broadcast_to(jnp.max(top, axis=1, keepdims=True), old.shape))
        fade = jnp.exp2(old - new)
        total = l_scr[...] * fade
        accum = acc_scr[...] * fade
        for mem, crel, slot in chunks:
            j = 16 + crel * 2 + slot if mem else crel * 8 + slot
            values = mem_rows(crel, slot, MV0) if mem else both(g1, crel, slot, V0, 128)
            p = jnp.exp2(s_buf[j] - jnp.concatenate([new, new], axis=1))
            total = total + p[:, :128] + p[:, 128:]
            high = p.astype(BF16)
            low = (p - high.astype(F32)).astype(BF16)
            accum = accum + dot_nn(high, values) + dot_nn(low, values)
        m_scr[...] = new
        l_scr[...] = total
        acc_scr[...] = accum

    def late(step):
        if step > 3 - LAG:
            advance(1, step)

    def take_sib(phase, *slots):
        for slot in slots:
            sib(phase, slot).wait_recv()

    absorb([(0, 0, 0)])
    pl.semaphore_wait(hello.at[0], 1)
    pl.semaphore_signal(hello.at[1], inc=1, device_id=row_dev, device_id_type=MESH)
    advance(0, 0)
    follow(0)
    absorb([(0, 0, 1), (0, 0, 2)])
    take_sib(0, 0)
    absorb([(0, 1, 0)])
    advance(0, 1)
    follow(1)
    absorb([(0, 0, 3), (0, 0, 4)])
    take_sib(0, 1, 2)
    absorb([(0, 1, 1), (0, 1, 2)])
    advance(0, 2)
    follow(2)
    absorb([(0, 0, 5), (0, 0, 6), (1, 0, 0)])
    take_sib(0, 3, 4)
    absorb([(0, 1, 3), (0, 1, 4)])
    advance(0, 3)
    follow(3)
    absorb([(0, 0, 7), (1, 0, 1)])
    take_sib(0, 5, 6)
    absorb([(0, 1, 5), (0, 1, 6), (1, 1, 0)])
    take_sib(0, 7)
    absorb([(0, 1, 7), (1, 1, 1)])

    total = jnp.broadcast_to(jnp.sum(l_scr[...], axis=1, keepdims=True), (256, 128))
    lse = m_scr[...] + jnp.log2(total)
    attended = (acc_scr[...] / total).astype(BF16)
    o_scr[...] = attended
    y_o = go(remote(o_scr, on_scr, y_ss.at[7], y_rs.at[7], y_dev))
    do_mine = both(g2, 0, 0, D0, 128)
    delta = jnp.broadcast_to(
        jnp.sum(do_mine.astype(F32) * attended.astype(F32), axis=1, keepdims=True), (256, 128)
    )
    m_scr[...] = lse
    l_scr[...] = delta
    eye = lax.broadcasted_iota(jnp.int32, (128, 128), 0) == lax.broadcasted_iota(
        jnp.int32, (128, 128), 1
    )
    ld[0, 0] = jnp.zeros((8, 256), F32)
    for yq in (0, 1):
        rows = slice(yq * 128, yq * 128 + 128)
        ld[0, 0, 0:1, rows] = jnp.sum(jnp.where(eye, lse[rows, :], 0.0), axis=0, keepdims=True)
        ld[0, 0, 1:2, rows] = jnp.sum(jnp.where(eye, delta[rows, :], 0.0), axis=0, keepdims=True)

    def ld_copy(off):
        slot = SLOT_OF[(-off) % NZ]
        return remote(
            ld.at[0, 0], ld.at[0, slot], ld_ss.at[slot - 1], ld_rs.at[slot - 1], at(i, z_at(off), core)
        )

    for off in (4, 3, 5, 2, 6, 1, 7):
        go(ld_copy(off))
    late(0)

    dq_scr[...] = jnp.zeros_like(dq_scr)

    def query_step(j, keys, values):
        p = jnp.exp2(s_buf[j] - jnp.concatenate([m_scr[...], m_scr[...]], axis=1))
        dp = dot_nt(do_mine, values)
        ds = (p * (dp - jnp.concatenate([l_scr[...], l_scr[...]], axis=1))).astype(BF16)
        dq_scr[...] += dot_nn(ds, keys)

    def query_loop(slot, carry):
        for crel in (0, 1):
            query_step(
                crel * 8 + slot, both(g1, crel, slot, K0, 128), both(g1, crel, slot, V0, 128)
            )
        return carry

    lax.fori_loop(0, 3, query_loop, 0)
    late(1)
    lax.fori_loop(3, 5, query_loop, 0)

    y_o.wait_recv()
    att_scr2 = jnp.concatenate([on_scr[128:256, :], on_scr[0:128, :]], axis=0)
    pair = (o_scr[...], att_scr2)
    att_t = jnp.concatenate(
        [
            jnp.where(i == 0, pair[0].astype(F32), pair[1].astype(F32)).T,
            jnp.where(i == 0, pair[1].astype(F32), pair[0].astype(F32)).T,
        ],
        axis=0,
    ).astype(BF16)
    y_og.wait_recv()

    def gw_part(k, cc):
        col = (z_at(k) * 2 + cc) * HD
        grads_in = jnp.concatenate(
            [
                og_buf[:, pl.ds(pl.multiple_of(i * half + col, HD), HD)],
                ogx[:, pl.ds(pl.multiple_of(col, HD), HD)],
            ],
            axis=0,
        )
        return dot_nn(att_t, grads_in)

    gw_sib = []
    for place, k in enumerate(GW_ORDER):
        gs_send[place] = gw_part(k, 1 - core).astype(BF16)
        if place % 4 == 3:
            cut = slice(place - 3, place + 1)
            n = 8 if place == 3 else 13
            gw_sib.append(
                go(remote(gs_send.at[cut], gs_recv.at[cut], y_ss.at[n], y_rs.at[n], sib_dev))
            )
    for place, k in enumerate(GW_ORDER):
        gw_acc[place] = gw_part(k, core)
    pl.semaphore_wait(hello.at[1], 1)
    att_scr[i] = o_scr[0:128, :]
    att_scr[1 - i] = on_scr[128:256, :]
    att_own = jnp.concatenate([att_scr[0], att_scr[1]], axis=1)
    width = w_hbm.shape[1] // heads_n

    def lo_copy(k):
        return remote(
            lo_send.at[k - 1],
            lo_recv.at[k - 1],
            lo_ss.at[k - 1],
            lo_rs.at[k - 1],
            {"head": lax.rem(head + k, heads_n)},
        )

    for k in list(range(1, heads_n)) + [0]:
        cols = pl.ds(pl.multiple_of(lax.rem(head + k, heads_n) * width, HD), width)
        part = dot_nn(att_own, w_buf[:, cols])
        if k:
            lo_send[k - 1] = part.astype(BF16)
            go(lo_copy(k))
        else:
            lo_own[...] = part
    late(2)

    def gw_copy(k):
        return remote(
            gw_send.at[k - 1],
            gw_recv.at[k - 1],
            gw_ss.at[k - 1],
            gw_rs.at[k - 1],
            at(i, z_at(k), core),
        )

    for place, k in enumerate(GW_ORDER):
        if place % 4 == 0:
            gw_sib[place // 4].wait_recv()
        block = gw_acc[place] + gs_recv[place].astype(F32)
        if k:
            gw_send[k - 1] = block.astype(BF16)
            go(gw_copy(k))
        else:
            gw_acc[0] = block

    for off in range(1, NZ):
        ld_copy(off).wait_recv()
    ld_sib = go(remote(ld.at[0], ld.at[1], y_ss.at[9], y_rs.at[9], sib_dev))
    lax.fori_loop(5, NZ, query_loop, 0)
    for crel in (0, 1):
        for group in (0, 1):
            query_step(
                16 + crel * 2 + group, mem_rows(crel, group, MK0), mem_rows(crel, group, MV0)
            )
    finish = []

    def give(kind, out, value):
        grads[kind] = value.astype(BF16)
        copy = pltpu.make_async_copy(grads.at[kind, 0:128], out.at[:, own_cols], out_sem.at[kind])
        copy.start()
        finish.append(copy)
        return go(
            remote(
                grads.at[kind, 128:256],
                out.at[:, own_cols],
                y_ss.at[10 + kind],
                y_rs.at[10 + kind],
                y_dev,
            )
        )

    given = [give(0, gq_out, dq_scr[...] * scale)]
    ld_sib.wait_recv()
    take_sib(1, *range(5))

    k_mine = both(g1, 0, 0, K0, 128)
    v_mine = both(g1, 0, 0, V0, 128)
    dk_scr[...] = jnp.zeros_like(dk_scr)
    dv_scr[...] = jnp.zeros_like(dv_scr)

    def key_step(crel, slot):
        queries = both(g2, crel, slot, Q0, 128)
        grad_out = both(g2, crel, slot, D0, 128)
        lse_row = ld[crel, slot, 0:1, :]
        delta_row = ld[crel, slot, 1:2, :]
        s = dot_nt(k_mine, queries) * (scale * LOG2E)
        rows = []
        for yk in (0, 1):
            row = []
            for yq in (0, 1):
                bias = jnp.where(
                    mask_ref[block_of(yq, slot, crel), own_blocks[yk]] > 0, 0.0, -jnp.inf
                )
                cut = slice(yq * 128, yq * 128 + 128)
                row.append(
                    jnp.exp2(s[yk * 128 : yk * 128 + 128, cut] + (bias - lse_row[:, cut]))
                )
            rows.append(jnp.concatenate(row, axis=1))
        p = jnp.concatenate(rows, axis=0)
        dp = dot_nt(v_mine, grad_out)
        ds = (p * (dp - delta_row)).astype(BF16)
        dv_scr[...] += dot_nn(p.astype(BF16), grad_out)
        dk_scr[...] += dot_nn(ds, queries)

    def key_steps(*slots):
        for slot in slots:
            for crel in (0, 1):
                key_step(crel, slot)

    key_steps(0, 1, 2, 3, 4)
    late(3)
    take_sib(1, 5, 6)
    key_steps(5, 6)
    take_sib(1, 7)
    key_steps(7)
    given.append(give(1, gk_out, dk_scr[...] * scale))
    given.append(give(2, gv_out, dv_scr[...]))

    result = lo_own[...]
    for k in range(1, heads_n):
        lo_copy(k).wait_recv()
        result = result + lo_recv[k - 1].astype(F32)
    lo_stage[...] = result.astype(BF16)
    copy = pltpu.make_async_copy(lo_stage, lo_out, out_sem.at[3])
    copy.start()
    finish.append(copy)
    result = gw_acc[0]
    for k in range(1, NZ):
        gw_copy(k).wait_recv()
        result = result + gw_recv[k - 1].astype(F32)
    gw_stage[...] = result.astype(BF16)
    copy = pltpu.make_async_copy(gw_stage, gw_out, out_sem.at[4])
    copy.start()
    finish.append(copy)

    for copy in given:
        copy.wait_recv()
    for copy in finish:
        copy.wait()
    for copy in started:
        copy.wait_send()


def hand_out(*refs):
    ins, outs, held, sems = refs[:5], refs[5:10], refs[10:15], refs[15]
    reads = [pltpu.make_async_copy(ins[n], held[n], sems.at[0, n]) for n in range(5)]
    writes = [pltpu.make_async_copy(held[n], outs[n], sems.at[1, n]) for n in range(5)]
    for copy in reads:
        copy.start()
    for n in range(5):
        reads[n].wait()
        writes[n].start()
    for copy in writes:
        copy.wait()


def per_device(
    queries,
    key_states,
    value_states,
    memory_keys,
    memory_values,
    memory_length,
    block_mask,
    out_weight,
    out_grad,
    *,
    heads_n,
):
    rows, cols = queries.shape
    d_model = out_weight.shape[1]
    width = d_model // heads_n
    hbm = pl.BlockSpec(memory_space=pltpu.HBM)
    smem = pl.BlockSpec(memory_space=pltpu.SMEM)
    vm = pltpu.VMEM
    dma = pltpu.SemaphoreType.DMA
    grad_shape = jax.ShapeDtypeStruct((rows, cols), BF16)
    results = pl.pallas_call(
        functools.partial(kernel, heads_n),
        out_shape=(
            jax.ShapeDtypeStruct((rows, width), BF16),
            jax.ShapeDtypeStruct((cols, HD), BF16),
            grad_shape,
            grad_shape,
            grad_shape,
        ),
        in_specs=[smem, smem] + [hbm] * 7,
        out_specs=(hbm,) * 5,
        scratch_shapes=[
            vm((2, NZ, 2, ROWS1, HD), BF16),
            vm((2, NZ, 2, ROWS2, HD), BF16),
            vm((20, 256, 256), F32),
            vm((cols, d_model), BF16),
            vm((rows, d_model), BF16),
            vm((rows, d_model // 2), BF16),
            vm((2, rows, HD), BF16),
            vm((256, HD), BF16),
            vm((256, HD), BF16),
            vm((2, rows, HD), BF16),
            vm((2, NZ, 8, 256), F32),
            vm((rows, width), F32),
            vm((max(heads_n - 1, 1), rows, width), BF16),
            vm((max(heads_n - 1, 1), rows, width), BF16),
            vm((NZ, 256, HD), BF16),
            vm((NZ, 256, HD), BF16),
            vm((NZ, 256, HD), F32),
            vm((NZ - 1, 256, HD), BF16),
            vm((NZ - 1, 256, HD), BF16),
            vm((256, HD), F32),
            vm((256, HD), F32),
            vm((256, HD), F32),
            vm((256, HD), F32),
            vm((256, HD), F32),
            vm((256, HD), F32),
            vm((3, 256, HD), BF16),
            vm((rows, width), BF16),
            vm((cols, HD), BF16),
            dma((7,)),
            dma((2, 2, 4, 2)),
            dma((2, 2, 4, 2)),
            dma((2, NZ)),
            dma((2, NZ)),
            dma((14,)),
            dma((14,)),
            dma((NZ - 1,)),
            dma((NZ - 1,)),
            dma((max(heads_n - 1, 1),)),
            dma((max(heads_n - 1, 1),)),
            dma((NZ - 1,)),
            dma((NZ - 1,)),
            dma((5,)),
            pltpu.SemaphoreType.REGULAR((2,)),
        ],
        compiler_params=pltpu.CompilerParams(
            collective_id=0, has_side_effects=True, vmem_limit_bytes=56 * 1024 * 1024
        ),
        name="attention",
    )(
        memory_length,
        block_mask,
        queries,
        key_states,
        value_states,
        memory_keys,
        memory_values,
        out_weight,
        out_grad,
    )
    return pl.pallas_call(
        hand_out,
        out_shape=tuple(jax.ShapeDtypeStruct(r.shape, r.dtype) for r in results),
        in_specs=[hbm] * 5,
        out_specs=(hbm,) * 5,
        scratch_shapes=[vm(r.shape, r.dtype) for r in results] + [dma((2, 5))],
        name="results",
    )(*results)


def solution(mesh):
    in_specs = (
        P("ctx", "head"),
        P("ctx", "head"),
        P("ctx", "head"),
        P("ctx", "head"),
        P("ctx", "head"),
        P(),
        P(),
        P("head", None),
        P("ctx", None),
    )
    out_specs = (
        P("ctx", "head"),
        P("head", "ctx"),
        P("ctx", "head"),
        P("ctx", "head"),
        P("ctx", "head"),
    )
    return jax.shard_map(
        functools.partial(per_device, heads_n=mesh.shape["head"]),
        mesh=mesh,
        in_specs=in_specs,
        out_specs=out_specs,
        check_vma=False,
    )
```

```python
import functools
import math

import jax
import jax.numpy as jnp
from jax import lax
from jax.experimental import pallas as pl
from jax.experimental.pallas import tpu as pltpu
from jax.sharding import PartitionSpec as P

HD = 128
BLK = 128
NZ = 8
NX = 4
LAG = 3
GW_ORDER = (4, 3, 5, 2, 6, 1, 7, 0)
F32 = jnp.float32
BF16 = jnp.bfloat16
MESH = pl.DeviceIdType.MESH
LOG2E = 1.4426950408889634

OFFSET = (0, -1, 1, -2, 2, -3, 3, 4)
SLOT_OF = {off % NZ: slot for slot, off in enumerate(OFFSET)}

K0, V0, MK0, MV0, ROWS1 = 0, 128, 256, 288, 320
Q0, D0, ROWS2 = 0, 128, 256


def dot_nt(a, b):
    return lax.dot_general(a, b, (((1,), (1,)), ((), ())), preferred_element_type=F32)


def dot_nn(a, b):
    return lax.dot_general(a, b, (((1,), (0,)), ((), ())), preferred_element_type=F32)


def kernel(
    heads_n,
    len_ref,
    mask_ref,
    q_hbm,
    k_hbm,
    v_hbm,
    mk_hbm,
    mv_hbm,
    w_hbm,
    og_hbm,
    lo_out,
    gw_out,
    gq_out,
    gk_out,
    gv_out,
    g1,
    g2,
    s_buf,
    w_buf,
    og_buf,
    ogx,
    do_scr,
    o_scr,
    on_scr,
    att_scr,
    ld,
    lo_own,
    lo_send,
    lo_recv,
    gs_send,
    gs_recv,
    gw_acc,
    gw_send,
    gw_recv,
    m_scr,
    l_scr,
    acc_scr,
    dq_scr,
    dk_scr,
    dv_scr,
    grads,
    lo_stage,
    gw_stage,
    local_sem,
    ring_ss,
    ring_rs,
    sib_ss,
    sib_rs,
    y_ss,
    y_rs,
    ld_ss,
    ld_rs,
    lo_ss,
    lo_rs,
    gw_ss,
    gw_rs,
    out_sem,
    hello,
):
    ctx = lax.axis_index("ctx")
    head = lax.axis_index("head")
    core = lax.rem(ctx, 2)
    z = lax.rem(ctx // 2, NZ)
    i = ctx // (2 * NZ)
    scale = 1.0 / math.sqrt(HD)

    def at(ii, zz, cc):
        return {"ctx": (ii * NZ + zz) * 2 + cc}

    def z_at(off):
        return lax.rem(z + (off % NZ), NZ)

    y_dev = at(1 - i, z, core)
    sib_dev = at(i, z, 1 - core)
    own_cols = pl.ds(pl.multiple_of(i * HD, HD), HD)
    other_cols = pl.ds(pl.multiple_of((1 - i) * HD, HD), HD)
    gather = (g1, g2)
    started = []

    def remote(src, dst, ss, rs, dev):
        return pltpu.make_async_remote_copy(
            src_ref=src, dst_ref=dst, send_sem=ss, recv_sem=rs, device_id=dev, device_id_type=MESH
        )

    def go(copy):
        copy.start()
        started.append(copy)
        return copy

    piece = g1.at[0, 0, 0]
    local1 = [
        pltpu.make_async_copy(k_hbm.at[:, own_cols], piece.at[K0 : K0 + 128], local_sem.at[0]),
        pltpu.make_async_copy(v_hbm.at[:, own_cols], piece.at[V0 : V0 + 128], local_sem.at[1]),
        pltpu.make_async_copy(mk_hbm.at[:, own_cols], piece.at[MK0 : MK0 + 32], local_sem.at[2]),
        pltpu.make_async_copy(mv_hbm.at[:, own_cols], piece.at[MV0 : MV0 + 32], local_sem.at[3]),
    ]
    local_q = pltpu.make_async_copy(
        q_hbm.at[:, own_cols], g2.at[0, 0, 0, Q0 : Q0 + 128], local_sem.at[4]
    )
    local_w = pltpu.make_async_copy(w_hbm, w_buf, local_sem.at[5])
    local_og = pltpu.make_async_copy(og_hbm, og_buf, local_sem.at[6])
    for copy in local1:
        copy.start()
    local_q.start()
    local_og.start()
    local_w.start()

    barrier = pltpu.get_barrier_semaphore()
    x = lax.rem(head, NX)
    row = head - x
    x_next = {"head": row + lax.rem(x + 1, NX)}
    x_last = {"head": row + lax.rem(x + NX - 1, NX)}
    row_dev = {"head": lax.rem(head + NX, heads_n)}
    peers = [y_dev, sib_dev, at(i, z_at(1), core), at(i, z_at(-1), core), x_next, x_last, row_dev]
    for dev in peers:
        pl.semaphore_signal(barrier, inc=1, device_id=dev, device_id_type=MESH)

    pl.semaphore_wait(barrier, len(peers))

    far = g1.at[0, 0, 1]
    y_first = [
        remote(k_hbm.at[:, other_cols], far.at[K0 : K0 + 128], y_ss.at[0], y_rs.at[0], y_dev),
        remote(v_hbm.at[:, other_cols], far.at[V0 : V0 + 128], y_ss.at[1], y_rs.at[1], y_dev),
        remote(mk_hbm.at[:, other_cols], far.at[MK0 : MK0 + 32], y_ss.at[2], y_rs.at[2], y_dev),
        remote(mv_hbm.at[:, other_cols], far.at[MV0 : MV0 + 32], y_ss.at[3], y_rs.at[3], y_dev),
    ]
    y_q = remote(
        q_hbm.at[:, other_cols], g2.at[0, 0, 1, Q0 : Q0 + 128], y_ss.at[4], y_rs.at[4], y_dev
    )

    def ring(phase, way, step, part):
        src = 0 if step == 0 else 2 * step - 1 + way
        dst = 7 if step == 3 else 2 * step + 1 + way
        buf = gather[phase]
        return remote(
            buf.at[0, src, part],
            buf.at[0, dst, part],
            ring_ss.at[phase, way, step, part],
            ring_rs.at[phase, way, step, part],
            at(i, z_at(1 if way == 0 else -1), core),
        )

    def ring_send(phase, step, part):
        for way in (0, 1):
            if step < 3 or part == way:
                go(ring(phase, way, step, part))

    def sib(phase, slot):
        buf = gather[phase]
        return remote(
            buf.at[0, slot], buf.at[1, slot], sib_ss.at[phase, slot], sib_rs.at[phase, slot], sib_dev
        )

    def follow(step):
        if step == 1:
            if LAG == 0:
                local_q.wait()
            ring_send(1, 0, 0)
            if LAG == 0:
                y_q.wait_recv()
            y_do.wait_recv()
            ring_send(1, 0, 1)
            go(sib(1, 0))
        if step >= LAG:
            advance(1, step - LAG)

    def take(phase, step, part):
        for way in (0, 1):
            ring(phase, way, step, part).wait_recv()
            if step < 2 or part == way:
                go(ring(phase, way, step + 1, part))

    def advance(phase, step):
        if step < 3:
            for part in (0, 1):
                if (phase, step, part) != (0, 0, 0):
                    take(phase, step, part)
            go(sib(phase, 2 * step + 1))
            go(sib(phase, 2 * step + 2))
        else:
            ring(phase, 0, 3, 0).wait_recv()
            ring(phase, 1, 3, 1).wait_recv()
            go(sib(phase, 7))

    for copy in local1:
        copy.wait()
    ring_send(0, 0, 0)
    for copy in y_first:
        go(copy)
    go(y_q)
    pl.semaphore_signal(hello.at[0], inc=1, device_id=x_next, device_id_type=MESH)

    local_og.wait()
    local_w.wait()
    grad_att = dot_nt(og_buf[...], w_buf[...]).astype(BF16)
    do_scr[0] = grad_att[:, :HD]
    do_scr[1] = grad_att[:, HD:]
    g2[0, 0, 0, D0 : D0 + 128, :] = do_scr[i]
    y_do = go(
        remote(do_scr.at[1 - i], g2.at[0, 0, 1, D0 : D0 + 128], y_ss.at[5], y_rs.at[5], y_dev)
    )
    take(0, 0, 0)
    for copy in y_first:
        copy.wait_recv()
    ring_send(0, 0, 1)
    go(sib(0, 0))
    half = og_hbm.shape[1] // 2
    y_og = go(
        remote(
            og_hbm.at[:, pl.ds(pl.multiple_of((1 - i) * half, HD), half)],
            ogx,
            y_ss.at[6],
            y_rs.at[6],
            y_dev,
        )
    )
    follow(-1)
    if LAG > 0:
        local_q.wait()
        y_q.wait_recv()

    def block_of(part, slot, crel):
        ii = i if part == 0 else 1 - i
        cc = core if crel == 0 else 1 - core
        return (ii * NZ + z_at(OFFSET[slot])) * 2 + cc

    own_blocks = [block_of(0, 0, 0), block_of(1, 0, 0)]

    def both(buf, crel, slot, row, rows):
        return jnp.concatenate(
            [buf[crel, slot, 0, row : row + rows, :], buf[crel, slot, 1, row : row + rows, :]], axis=0
        )

    q_mine = both(g2, 0, 0, Q0, 128)
    m_scr[...] = jnp.full_like(m_scr, -jnp.inf)
    l_scr[...] = jnp.zeros_like(l_scr)
    acc_scr[...] = jnp.zeros_like(acc_scr)
    lane = lax.broadcasted_iota(jnp.int32, (1, 256), 1)

    def seq_scores(crel, slot):
        s = dot_nt(q_mine, both(g1, crel, slot, K0, 128)) * (scale * LOG2E)
        top = None
        for yq in (0, 1):
            row = []
            for yk in (0, 1):
                bias = jnp.where(
                    mask_ref[own_blocks[yq], block_of(yk, slot, crel)] > 0, 0.0, -jnp.inf
                )
                row.append(s[yq * 128 : yq * 128 + 128, yk * 128 : yk * 128 + 128] + bias)
                s_buf[crel * 8 + slot, yq * 128 : yq * 128 + 128, yk * 128 : yk * 128 + 128] = row[yk]
            both_k = jnp.maximum(row[0], row[1])
            top = both_k if top is None else jnp.concatenate([top, both_k], axis=0)
        return top

    def mem_rows(crel, group, row):
        return jnp.concatenate(
            [
                g1[crel, slot, part, row : row + 32, :]
                for slot in range(4 * group, 4 * group + 4)
                for part in (0, 1)
            ],
            axis=0,
        )

    def mem_scores(crel, group):
        s = dot_nt(q_mine, mem_rows(crel, group, MK0)) * (scale * LOG2E)
        base = jnp.zeros((1, 256), jnp.int32)
        place = 0
        for slot in range(4 * group, 4 * group + 4):
            for part in (0, 1):
                base = jnp.where(lane // 32 == place, block_of(part, slot, crel), base)
                place += 1
        index = base * 32 + lane % 32
        top = []
        for yq in (0, 1):
            allow = index < len_ref[own_blocks[yq]]
            t = jnp.where(allow, s[yq * 128 : yq * 128 + 128, :], -jnp.inf)
            s_buf[16 + crel * 2 + group, yq * 128 : yq * 128 + 128, :] = t
            top.append(jnp.maximum(t[:, :128], t[:, 128:]))
        return jnp.concatenate(top, axis=0)

    def absorb(chunks):
        tops = [mem_scores(*c[1:]) if c[0] else seq_scores(*c[1:]) for c in chunks]
        top = functools.reduce(jnp.maximum, tops)
        old = m_scr[...]
        new = jnp.maximum(old, jnp.broadcast_to(jnp.max(top, axis=1, keepdims=True), old.shape))
        fade = jnp.exp2(old - new)
        total = l_scr[...] * fade
        accum = acc_scr[...] * fade
        for mem, crel, slot in chunks:
            j = 16 + crel * 2 + slot if mem else crel * 8 + slot
            values = mem_rows(crel, slot, MV0) if mem else both(g1, crel, slot, V0, 128)
            p = jnp.exp2(s_buf[j] - jnp.concatenate([new, new], axis=1))
            total = total + p[:, :128] + p[:, 128:]
            high = p.astype(BF16)
            low = (p - high.astype(F32)).astype(BF16)
            accum = accum + dot_nn(high, values) + dot_nn(low, values)
        m_scr[...] = new
        l_scr[...] = total
        acc_scr[...] = accum

    def late(step):
        if step > 3 - LAG:
            advance(1, step)

    def take_sib(phase, *slots):
        for slot in slots:
            sib(phase, slot).wait_recv()

    absorb([(0, 0, 0)])
    pl.semaphore_wait(hello.at[0], 1)
    pl.semaphore_signal(hello.at[1], inc=1, device_id=row_dev, device_id_type=MESH)
    advance(0, 0)
    follow(0)
    absorb([(0, 0, 1), (0, 0, 2)])
    take_sib(0, 0)
    absorb([(0, 1, 0)])
    advance(0, 1)
    follow(1)
    absorb([(0, 0, 3), (0, 0, 4)])
    take_sib(0, 1, 2)
    absorb([(0, 1, 1), (0, 1, 2)])
    advance(0, 2)
    follow(2)
    absorb([(0, 0, 5), (0, 0, 6), (1, 0, 0)])
    take_sib(0, 3, 4)
    absorb([(0, 1, 3), (0, 1, 4)])
    advance(0, 3)
    follow(3)
    absorb([(0, 0, 7), (1, 0, 1)])
    take_sib(0, 5, 6)
    absorb([(0, 1, 5), (0, 1, 6), (1, 1, 0)])
    take_sib(0, 7)
    absorb([(0, 1, 7), (1, 1, 1)])

    total = jnp.broadcast_to(jnp.sum(l_scr[...], axis=1, keepdims=True), (256, 128))
    lse = m_scr[...] + jnp.log2(total)
    attended = (acc_scr[...] / total).astype(BF16)
    o_scr[...] = attended
    y_o = go(remote(o_scr, on_scr, y_ss.at[7], y_rs.at[7], y_dev))
    do_mine = both(g2, 0, 0, D0, 128)
    delta = jnp.broadcast_to(
        jnp.sum(do_mine.astype(F32) * attended.astype(F32), axis=1, keepdims=True), (256, 128)
    )
    m_scr[...] = lse
    l_scr[...] = delta
    eye = lax.broadcasted_iota(jnp.int32, (128, 128), 0) == lax.broadcasted_iota(
        jnp.int32, (128, 128), 1
    )
    ld[0, 0] = jnp.zeros((8, 256), F32)
    for yq in (0, 1):
        rows = slice(yq * 128, yq * 128 + 128)
        ld[0, 0, 0:1, rows] = jnp.sum(jnp.where(eye, lse[rows, :], 0.0), axis=0, keepdims=True)
        ld[0, 0, 1:2, rows] = jnp.sum(jnp.where(eye, delta[rows, :], 0.0), axis=0, keepdims=True)

    def ld_copy(off):
        slot = SLOT_OF[(-off) % NZ]
        return remote(
            ld.at[0, 0], ld.at[0, slot], ld_ss.at[slot - 1], ld_rs.at[slot - 1], at(i, z_at(off), core)
        )

    for off in (4, 3, 5, 2, 6, 1, 7):
        go(ld_copy(off))
    late(0)

    dq_scr[...] = jnp.zeros_like(dq_scr)

    def query_step(j, keys, values):
        p = jnp.exp2(s_buf[j] - jnp.concatenate([m_scr[...], m_scr[...]], axis=1))
        dp = dot_nt(do_mine, values)
        ds = (p * (dp - jnp.concatenate([l_scr[...], l_scr[...]], axis=1))).astype(BF16)
        dq_scr[...] += dot_nn(ds, keys)

    def query_loop(slot, carry):
        for crel in (0, 1):
            query_step(
                crel * 8 + slot, both(g1, crel, slot, K0, 128), both(g1, crel, slot, V0, 128)
            )
        return carry

    lax.fori_loop(0, 2, query_loop, 0)
    late(1)
    lax.fori_loop(2, 4, query_loop, 0)

    y_o.wait_recv()
    att_scr2 = jnp.concatenate([on_scr[128:256, :], on_scr[0:128, :]], axis=0)
    pair = (o_scr[...], att_scr2)
    att_t = jnp.concatenate(
        [
            jnp.where(i == 0, pair[0].astype(F32), pair[1].astype(F32)).T,
            jnp.where(i == 0, pair[1].astype(F32), pair[0].astype(F32)).T,
        ],
        axis=0,
    ).astype(BF16)
    y_og.wait_recv()

    def gw_part(k, cc):
        col = (z_at(k) * 2 + cc) * HD
        grads_in = jnp.concatenate(
            [
                og_buf[:, pl.ds(pl.multiple_of(i * half + col, HD), HD)],
                ogx[:, pl.ds(pl.multiple_of(col, HD), HD)],
            ],
            axis=0,
        )
        return dot_nn(att_t, grads_in)

    gw_sib = []
    for place, k in enumerate(GW_ORDER):
        gs_send[place] = gw_part(k, 1 - core).astype(BF16)
        if place % 4 == 3:
            cut = slice(place - 3, place + 1)
            n = 8 if place == 3 else 13
            gw_sib.append(
                go(remote(gs_send.at[cut], gs_recv.at[cut], y_ss.at[n], y_rs.at[n], sib_dev))
            )
    for place, k in enumerate(GW_ORDER):
        gw_acc[place] = gw_part(k, core)
    pl.semaphore_wait(hello.at[1], 1)
    att_scr[i] = o_scr[0:128, :]
    att_scr[1 - i] = on_scr[128:256, :]
    att_own = jnp.concatenate([att_scr[0], att_scr[1]], axis=1)
    width = w_hbm.shape[1] // heads_n

    def lo_copy(k):
        return remote(
            lo_send.at[k - 1],
            lo_recv.at[k - 1],
            lo_ss.at[k - 1],
            lo_rs.at[k - 1],
            {"head": lax.rem(head + k, heads_n)},
        )

    for k in list(range(1, heads_n)) + [0]:
        cols = pl.ds(pl.multiple_of(lax.rem(head + k, heads_n) * width, HD), width)
        part = dot_nn(att_own, w_buf[:, cols])
        if k:
            lo_send[k - 1] = part.astype(BF16)
            go(lo_copy(k))
        else:
            lo_own[...] = part
    late(2)

    def gw_copy(k):
        return remote(
            gw_send.at[k - 1],
            gw_recv.at[k - 1],
            gw_ss.at[k - 1],
            gw_rs.at[k - 1],
            at(i, z_at(k), core),
        )

    for place, k in enumerate(GW_ORDER):
        if place % 4 == 0:
            gw_sib[place // 4].wait_recv()
        block = gw_acc[place] + gs_recv[place].astype(F32)
        if k:
            gw_send[k - 1] = block.astype(BF16)
            go(gw_copy(k))
        else:
            gw_acc[0] = block

    for off in range(1, NZ):
        ld_copy(off).wait_recv()
    ld_sib = go(remote(ld.at[0], ld.at[1], y_ss.at[9], y_rs.at[9], sib_dev))
    lax.fori_loop(4, NZ, query_loop, 0)
    for crel in (0, 1):
        for group in (0, 1):
            query_step(
                16 + crel * 2 + group, mem_rows(crel, group, MK0), mem_rows(crel, group, MV0)
            )
    finish = []

    def give(kind, out, value):
        grads[kind] = value.astype(BF16)
        copy = pltpu.make_async_copy(grads.at[kind, 0:128], out.at[:, own_cols], out_sem.at[kind])
        copy.start()
        finish.append(copy)
        return go(
            remote(
                grads.at[kind, 128:256],
                out.at[:, own_cols],
                y_ss.at[10 + kind],
                y_rs.at[10 + kind],
                y_dev,
            )
        )

    given = [give(0, gq_out, dq_scr[...] * scale)]
    ld_sib.wait_recv()
    take_sib(1, *range(5))

    k_mine = both(g1, 0, 0, K0, 128)
    v_mine = both(g1, 0, 0, V0, 128)
    dk_scr[...] = jnp.zeros_like(dk_scr)
    dv_scr[...] = jnp.zeros_like(dv_scr)

    def key_step(crel, slot):
        queries = both(g2, crel, slot, Q0, 128)
        grad_out = both(g2, crel, slot, D0, 128)
        lse_row = ld[crel, slot, 0:1, :]
        delta_row = ld[crel, slot, 1:2, :]
        s = dot_nt(k_mine, queries) * (scale * LOG2E)
        rows = []
        for yk in (0, 1):
            row = []
            for yq in (0, 1):
                bias = jnp.where(
                    mask_ref[block_of(yq, slot, crel), own_blocks[yk]] > 0, 0.0, -jnp.inf
                )
                cut = slice(yq * 128, yq * 128 + 128)
                row.append(
                    jnp.exp2(s[yk * 128 : yk * 128 + 128, cut] + (bias - lse_row[:, cut]))
                )
            rows.append(jnp.concatenate(row, axis=1))
        p = jnp.concatenate(rows, axis=0)
        dp = dot_nt(v_mine, grad_out)
        ds = (p * (dp - delta_row)).astype(BF16)
        dv_scr[...] += dot_nn(p.astype(BF16), grad_out)
        dk_scr[...] += dot_nn(ds, queries)

    def key_steps(*slots):
        for slot in slots:
            for crel in (0, 1):
                key_step(crel, slot)

    key_steps(0, 1, 2, 3, 4)
    late(3)
    take_sib(1, 5, 6)
    key_steps(5, 6)
    take_sib(1, 7)
    key_steps(7)
    given.append(give(1, gk_out, dk_scr[...] * scale))
    given.append(give(2, gv_out, dv_scr[...]))

    result = lo_own[...]
    for k in range(1, heads_n):
        lo_copy(k).wait_recv()
        result = result + lo_recv[k - 1].astype(F32)
    lo_stage[...] = result.astype(BF16)
    copy = pltpu.make_async_copy(lo_stage, lo_out, out_sem.at[3])
    copy.start()
    finish.append(copy)
    result = gw_acc[0]
    for k in range(1, NZ):
        gw_copy(k).wait_recv()
        result = result + gw_recv[k - 1].astype(F32)
    gw_stage[...] = result.astype(BF16)
    copy = pltpu.make_async_copy(gw_stage, gw_out, out_sem.at[4])
    copy.start()
    finish.append(copy)

    for copy in given:
        copy.wait_recv()
    for copy in finish:
        copy.wait()
    for copy in started:
        copy.wait_send()


def hand_out(*refs):
    ins, outs, held, sems = refs[:5], refs[5:10], refs[10:15], refs[15]
    reads = [pltpu.make_async_copy(ins[n], held[n], sems.at[0, n]) for n in range(5)]
    writes = [pltpu.make_async_copy(held[n], outs[n], sems.at[1, n]) for n in range(5)]
    for copy in reads:
        copy.start()
    for n in range(5):
        reads[n].wait()
        writes[n].start()
    for copy in writes:
        copy.wait()


def per_device(
    queries,
    key_states,
    value_states,
    memory_keys,
    memory_values,
    memory_length,
    block_mask,
    out_weight,
    out_grad,
    *,
    heads_n,
):
    rows, cols = queries.shape
    d_model = out_weight.shape[1]
    width = d_model // heads_n
    hbm = pl.BlockSpec(memory_space=pltpu.HBM)
    smem = pl.BlockSpec(memory_space=pltpu.SMEM)
    vm = pltpu.VMEM
    dma = pltpu.SemaphoreType.DMA
    grad_shape = jax.ShapeDtypeStruct((rows, cols), BF16)
    results = pl.pallas_call(
        functools.partial(kernel, heads_n),
        out_shape=(
            jax.ShapeDtypeStruct((rows, width), BF16),
            jax.ShapeDtypeStruct((cols, HD), BF16),
            grad_shape,
            grad_shape,
            grad_shape,
        ),
        in_specs=[smem, smem] + [hbm] * 7,
        out_specs=(hbm,) * 5,
        scratch_shapes=[
            vm((2, NZ, 2, ROWS1, HD), BF16),
            vm((2, NZ, 2, ROWS2, HD), BF16),
            vm((20, 256, 256), F32),
            vm((cols, d_model), BF16),
            vm((rows, d_model), BF16),
            vm((rows, d_model // 2), BF16),
            vm((2, rows, HD), BF16),
            vm((256, HD), BF16),
            vm((256, HD), BF16),
            vm((2, rows, HD), BF16),
            vm((2, NZ, 8, 256), F32),
            vm((rows, width), F32),
            vm((max(heads_n - 1, 1), rows, width), BF16),
            vm((max(heads_n - 1, 1), rows, width), BF16),
            vm((NZ, 256, HD), BF16),
            vm((NZ, 256, HD), BF16),
            vm((NZ, 256, HD), F32),
            vm((NZ - 1, 256, HD), BF16),
            vm((NZ - 1, 256, HD), BF16),
            vm((256, HD), F32),
            vm((256, HD), F32),
            vm((256, HD), F32),
            vm((256, HD), F32),
            vm((256, HD), F32),
            vm((256, HD), F32),
            vm((3, 256, HD), BF16),
            vm((rows, width), BF16),
            vm((cols, HD), BF16),
            dma((7,)),
            dma((2, 2, 4, 2)),
            dma((2, 2, 4, 2)),
            dma((2, NZ)),
            dma((2, NZ)),
            dma((14,)),
            dma((14,)),
            dma((NZ - 1,)),
            dma((NZ - 1,)),
            dma((max(heads_n - 1, 1),)),
            dma((max(heads_n - 1, 1),)),
            dma((NZ - 1,)),
            dma((NZ - 1,)),
            dma((5,)),
            pltpu.SemaphoreType.REGULAR((2,)),
        ],
        compiler_params=pltpu.CompilerParams(
            collective_id=0, has_side_effects=True, vmem_limit_bytes=56 * 1024 * 1024
        ),
        name="attention",
    )(
        memory_length,
        block_mask,
        queries,
        key_states,
        value_states,
        memory_keys,
        memory_values,
        out_weight,
        out_grad,
    )
    return pl.pallas_call(
        hand_out,
        out_shape=tuple(jax.ShapeDtypeStruct(r.shape, r.dtype) for r in results),
        in_specs=[hbm] * 5,
        out_specs=(hbm,) * 5,
        scratch_shapes=[vm(r.shape, r.dtype) for r in results] + [dma((2, 5))],
        name="results",
    )(*results)


def solution(mesh):
    in_specs = (
        P("ctx", "head"),
        P("ctx", "head"),
        P("ctx", "head"),
        P("ctx", "head"),
        P("ctx", "head"),
        P(),
        P(),
        P("head", None),
        P("ctx", None),
    )
    out_specs = (
        P("ctx", "head"),
        P("head", "ctx"),
        P("ctx", "head"),
        P("ctx", "head"),
        P("ctx", "head"),
    )
    return jax.shard_map(
        functools.partial(per_device, heads_n=mesh.shape["head"]),
        mesh=mesh,
        in_specs=in_specs,
        out_specs=out_specs,
        check_vma=False,
    )
```

```python
import functools
import math

import jax
import jax.numpy as jnp
from jax import lax
from jax.experimental import pallas as pl
from jax.experimental.pallas import tpu as pltpu
from jax.sharding import PartitionSpec as P

HD = 128
BLK = 128
NZ = 8
NX = 4
LAG = 3
GW_ORDER = (4, 3, 5, 2, 6, 1, 7, 0)
F32 = jnp.float32
BF16 = jnp.bfloat16
MESH = pl.DeviceIdType.MESH
LOG2E = 1.4426950408889634

OFFSET = (0, -1, 1, -2, 2, -3, 3, 4)
SLOT_OF = {off % NZ: slot for slot, off in enumerate(OFFSET)}

K0, V0, MK0, MV0, ROWS1 = 0, 128, 256, 288, 320
Q0, D0, ROWS2 = 0, 128, 256


def dot_nt(a, b):
    return lax.dot_general(a, b, (((1,), (1,)), ((), ())), preferred_element_type=F32)


def dot_nn(a, b):
    return lax.dot_general(a, b, (((1,), (0,)), ((), ())), preferred_element_type=F32)


def kernel(
    heads_n,
    len_ref,
    mask_ref,
    q_hbm,
    k_hbm,
    v_hbm,
    mk_hbm,
    mv_hbm,
    w_hbm,
    og_hbm,
    lo_out,
    gw_out,
    gq_out,
    gk_out,
    gv_out,
    g1,
    g2,
    s_buf,
    w_buf,
    og_buf,
    ogx,
    do_scr,
    o_scr,
    on_scr,
    att_scr,
    ld,
    lo_own,
    lo_send,
    lo_recv,
    gs_send,
    gs_recv,
    gw_acc,
    gw_send,
    gw_recv,
    m_scr,
    l_scr,
    acc_scr,
    dq_scr,
    dk_scr,
    dv_scr,
    grads,
    lo_stage,
    gw_stage,
    local_sem,
    ring_ss,
    ring_rs,
    sib_ss,
    sib_rs,
    y_ss,
    y_rs,
    ld_ss,
    ld_rs,
    lo_ss,
    lo_rs,
    gw_ss,
    gw_rs,
    out_sem,
    hello,
):
    ctx = lax.axis_index("ctx")
    head = lax.axis_index("head")
    core = lax.rem(ctx, 2)
    z = lax.rem(ctx // 2, NZ)
    i = ctx // (2 * NZ)
    scale = 1.0 / math.sqrt(HD)

    def at(ii, zz, cc):
        return {"ctx": (ii * NZ + zz) * 2 + cc}

    def z_at(off):
        return lax.rem(z + (off % NZ), NZ)

    y_dev = at(1 - i, z, core)
    sib_dev = at(i, z, 1 - core)
    own_cols = pl.ds(pl.multiple_of(i * HD, HD), HD)
    other_cols = pl.ds(pl.multiple_of((1 - i) * HD, HD), HD)
    gather = (g1, g2)
    started = []

    def remote(src, dst, ss, rs, dev):
        return pltpu.make_async_remote_copy(
            src_ref=src, dst_ref=dst, send_sem=ss, recv_sem=rs, device_id=dev, device_id_type=MESH
        )

    def go(copy):
        copy.start()
        started.append(copy)
        return copy

    piece = g1.at[0, 0, 0]
    local1 = [
        pltpu.make_async_copy(k_hbm.at[:, own_cols], piece.at[K0 : K0 + 128], local_sem.at[0]),
        pltpu.make_async_copy(v_hbm.at[:, own_cols], piece.at[V0 : V0 + 128], local_sem.at[1]),
        pltpu.make_async_copy(mk_hbm.at[:, own_cols], piece.at[MK0 : MK0 + 32], local_sem.at[2]),
        pltpu.make_async_copy(mv_hbm.at[:, own_cols], piece.at[MV0 : MV0 + 32], local_sem.at[3]),
    ]
    local_q = pltpu.make_async_copy(
        q_hbm.at[:, own_cols], g2.at[0, 0, 0, Q0 : Q0 + 128], local_sem.at[4]
    )
    local_w = pltpu.make_async_copy(w_hbm, w_buf, local_sem.at[5])
    local_og = pltpu.make_async_copy(og_hbm, og_buf, local_sem.at[6])
    for copy in local1:
        copy.start()
    local_q.start()
    local_og.start()
    local_w.start()

    barrier = pltpu.get_barrier_semaphore()
    x = lax.rem(head, NX)
    row = head - x
    x_next = {"head": row + lax.rem(x + 1, NX)}
    x_last = {"head": row + lax.rem(x + NX - 1, NX)}
    row_dev = {"head": lax.rem(head + NX, heads_n)}
    peers = [y_dev, sib_dev, at(i, z_at(1), core), at(i, z_at(-1), core), x_next, x_last, row_dev]
    for dev in peers:
        pl.semaphore_signal(barrier, inc=1, device_id=dev, device_id_type=MESH)

    pl.semaphore_wait(barrier, len(peers))

    far = g1.at[0, 0, 1]
    y_first = [
        remote(k_hbm.at[:, other_cols], far.at[K0 : K0 + 128], y_ss.at[0], y_rs.at[0], y_dev),
        remote(v_hbm.at[:, other_cols], far.at[V0 : V0 + 128], y_ss.at[1], y_rs.at[1], y_dev),
        remote(mk_hbm.at[:, other_cols], far.at[MK0 : MK0 + 32], y_ss.at[2], y_rs.at[2], y_dev),
        remote(mv_hbm.at[:, other_cols], far.at[MV0 : MV0 + 32], y_ss.at[3], y_rs.at[3], y_dev),
    ]
    y_q = remote(
        q_hbm.at[:, other_cols], g2.at[0, 0, 1, Q0 : Q0 + 128], y_ss.at[4], y_rs.at[4], y_dev
    )

    def ring(phase, way, step, part):
        src = 0 if step == 0 else 2 * step - 1 + way
        dst = 7 if step == 3 else 2 * step + 1 + way
        buf = gather[phase]
        return remote(
            buf.at[0, src, part],
            buf.at[0, dst, part],
            ring_ss.at[phase, way, step, part],
            ring_rs.at[phase, way, step, part],
            at(i, z_at(1 if way == 0 else -1), core),
        )

    def ring_send(phase, step, part):
        for way in (0, 1):
            if step < 3 or part == way:
                go(ring(phase, way, step, part))

    def sib(phase, slot):
        buf = gather[phase]
        return remote(
            buf.at[0, slot], buf.at[1, slot], sib_ss.at[phase, slot], sib_rs.at[phase, slot], sib_dev
        )

    def follow(step):
        if step == 1:
            if LAG == 0:
                local_q.wait()
            ring_send(1, 0, 0)
            if LAG == 0:
                y_q.wait_recv()
            y_do.wait_recv()
            ring_send(1, 0, 1)
            go(sib(1, 0))
        if step >= LAG:
            advance(1, step - LAG)

    def take(phase, step, part):
        for way in (0, 1):
            ring(phase, way, step, part).wait_recv()
            if step < 2 or part == way:
                go(ring(phase, way, step + 1, part))

    def advance(phase, step):
        if step < 3:
            for part in (0, 1):
                if (phase, step, part) != (0, 0, 0):
                    take(phase, step, part)
            go(sib(phase, 2 * step + 1))
            go(sib(phase, 2 * step + 2))
        else:
            ring(phase, 0, 3, 0).wait_recv()
            ring(phase, 1, 3, 1).wait_recv()
            go(sib(phase, 7))

    for copy in local1:
        copy.wait()
    ring_send(0, 0, 0)
    for copy in y_first:
        go(copy)
    go(y_q)
    pl.semaphore_signal(hello.at[0], inc=1, device_id=x_next, device_id_type=MESH)

    local_og.wait()
    local_w.wait()
    grad_att = dot_nt(og_buf[...], w_buf[...]).astype(BF16)
    do_scr[0] = grad_att[:, :HD]
    do_scr[1] = grad_att[:, HD:]
    g2[0, 0, 0, D0 : D0 + 128, :] = do_scr[i]
    y_do = go(
        remote(do_scr.at[1 - i], g2.at[0, 0, 1, D0 : D0 + 128], y_ss.at[5], y_rs.at[5], y_dev)
    )
    take(0, 0, 0)
    for copy in y_first:
        copy.wait_recv()
    ring_send(0, 0, 1)
    go(sib(0, 0))
    half = og_hbm.shape[1] // 2
    y_og = go(
        remote(
            og_hbm.at[:, pl.ds(pl.multiple_of((1 - i) * half, HD), half)],
            ogx,
            y_ss.at[6],
            y_rs.at[6],
            y_dev,
        )
    )
    follow(-1)
    if LAG > 0:
        local_q.wait()
        y_q.wait_recv()

    def block_of(part, slot, crel):
        ii = i if part == 0 else 1 - i
        cc = core if crel == 0 else 1 - core
        return (ii * NZ + z_at(OFFSET[slot])) * 2 + cc

    own_blocks = [block_of(0, 0, 0), block_of(1, 0, 0)]

    def both(buf, crel, slot, row, rows):
        return jnp.concatenate(
            [buf[crel, slot, 0, row : row + rows, :], buf[crel, slot, 1, row : row + rows, :]], axis=0
        )

    q_mine = both(g2, 0, 0, Q0, 128)
    m_scr[...] = jnp.full_like(m_scr, -jnp.inf)
    l_scr[...] = jnp.zeros_like(l_scr)
    acc_scr[...] = jnp.zeros_like(acc_scr)
    lane = lax.broadcasted_iota(jnp.int32, (1, 256), 1)

    def seq_scores(crel, slot):
        s = dot_nt(q_mine, both(g1, crel, slot, K0, 128)) * (scale * LOG2E)
        top = None
        for yq in (0, 1):
            row = []
            for yk in (0, 1):
                bias = jnp.where(
                    mask_ref[own_blocks[yq], block_of(yk, slot, crel)] > 0, 0.0, -jnp.inf
                )
                row.append(s[yq * 128 : yq * 128 + 128, yk * 128 : yk * 128 + 128] + bias)
                s_buf[crel * 8 + slot, yq * 128 : yq * 128 + 128, yk * 128 : yk * 128 + 128] = row[yk]
            both_k = jnp.maximum(row[0], row[1])
            top = both_k if top is None else jnp.concatenate([top, both_k], axis=0)
        return top

    def mem_rows(crel, group, row):
        return jnp.concatenate(
            [
                g1[crel, slot, part, row : row + 32, :]
                for slot in range(4 * group, 4 * group + 4)
                for part in (0, 1)
            ],
            axis=0,
        )

    def mem_scores(crel, group):
        s = dot_nt(q_mine, mem_rows(crel, group, MK0)) * (scale * LOG2E)
        base = jnp.zeros((1, 256), jnp.int32)
        place = 0
        for slot in range(4 * group, 4 * group + 4):
            for part in (0, 1):
                base = jnp.where(lane // 32 == place, block_of(part, slot, crel), base)
                place += 1
        index = base * 32 + lane % 32
        top = []
        for yq in (0, 1):
            allow = index < len_ref[own_blocks[yq]]
            t = jnp.where(allow, s[yq * 128 : yq * 128 + 128, :], -jnp.inf)
            s_buf[16 + crel * 2 + group, yq * 128 : yq * 128 + 128, :] = t
            top.append(jnp.maximum(t[:, :128], t[:, 128:]))
        return jnp.concatenate(top, axis=0)

    def absorb(chunks):
        tops = [mem_scores(*c[1:]) if c[0] else seq_scores(*c[1:]) for c in chunks]
        top = functools.reduce(jnp.maximum, tops)
        old = m_scr[...]
        new = jnp.maximum(old, jnp.broadcast_to(jnp.max(top, axis=1, keepdims=True), old.shape))
        fade = jnp.exp2(old - new)
        total = l_scr[...] * fade
        accum = acc_scr[...] * fade
        for mem, crel, slot in chunks:
            j = 16 + crel * 2 + slot if mem else crel * 8 + slot
            values = mem_rows(crel, slot, MV0) if mem else both(g1, crel, slot, V0, 128)
            p = jnp.exp2(s_buf[j] - jnp.concatenate([new, new], axis=1))
            total = total + p[:, :128] + p[:, 128:]
            high = p.astype(BF16)
            low = (p - high.astype(F32)).astype(BF16)
            accum = accum + dot_nn(high, values) + dot_nn(low, values)
        m_scr[...] = new
        l_scr[...] = total
        acc_scr[...] = accum

    def late(step):
        if step > 3 - LAG:
            advance(1, step)

    def take_sib(phase, *slots):
        for slot in slots:
            sib(phase, slot).wait_recv()

    absorb([(0, 0, 0)])
    pl.semaphore_wait(hello.at[0], 1)
    pl.semaphore_signal(hello.at[1], inc=1, device_id=row_dev, device_id_type=MESH)
    advance(0, 0)
    follow(0)
    absorb([(0, 0, 1), (0, 0, 2)])
    take_sib(0, 0)
    absorb([(0, 1, 0)])
    advance(0, 1)
    follow(1)
    absorb([(0, 0, 3), (0, 0, 4)])
    take_sib(0, 1, 2)
    absorb([(0, 1, 1), (0, 1, 2)])
    advance(0, 2)
    follow(2)
    absorb([(0, 0, 5), (0, 0, 6), (1, 0, 0)])
    take_sib(0, 3, 4)
    absorb([(0, 1, 3), (0, 1, 4)])
    follow(3)
    advance(0, 3)
    absorb([(0, 0, 7), (1, 0, 1)])
    take_sib(0, 5, 6)
    absorb([(0, 1, 5), (0, 1, 6), (1, 1, 0)])
    take_sib(0, 7)
    absorb([(0, 1, 7), (1, 1, 1)])

    total = jnp.broadcast_to(jnp.sum(l_scr[...], axis=1, keepdims=True), (256, 128))
    lse = m_scr[...] + jnp.log2(total)
    attended = (acc_scr[...] / total).astype(BF16)
    o_scr[...] = attended
    y_o = go(remote(o_scr, on_scr, y_ss.at[7], y_rs.at[7], y_dev))
    do_mine = both(g2, 0, 0, D0, 128)
    delta = jnp.broadcast_to(
        jnp.sum(do_mine.astype(F32) * attended.astype(F32), axis=1, keepdims=True), (256, 128)
    )
    m_scr[...] = lse
    l_scr[...] = delta
    eye = lax.broadcasted_iota(jnp.int32, (128, 128), 0) == lax.broadcasted_iota(
        jnp.int32, (128, 128), 1
    )
    ld[0, 0] = jnp.zeros((8, 256), F32)
    for yq in (0, 1):
        rows = slice(yq * 128, yq * 128 + 128)
        ld[0, 0, 0:1, rows] = jnp.sum(jnp.where(eye, lse[rows, :], 0.0), axis=0, keepdims=True)
        ld[0, 0, 1:2, rows] = jnp.sum(jnp.where(eye, delta[rows, :], 0.0), axis=0, keepdims=True)

    def ld_copy(off):
        slot = SLOT_OF[(-off) % NZ]
        return remote(
            ld.at[0, 0], ld.at[0, slot], ld_ss.at[slot - 1], ld_rs.at[slot - 1], at(i, z_at(off), core)
        )

    for off in (4, 3, 5, 2, 6, 1, 7):
        go(ld_copy(off))
    late(0)

    dq_scr[...] = jnp.zeros_like(dq_scr)

    def query_step(j, keys, values):
        p = jnp.exp2(s_buf[j] - jnp.concatenate([m_scr[...], m_scr[...]], axis=1))
        dp = dot_nt(do_mine, values)
        ds = (p * (dp - jnp.concatenate([l_scr[...], l_scr[...]], axis=1))).astype(BF16)
        dq_scr[...] += dot_nn(ds, keys)

    def query_loop(slot, carry):
        for crel in (0, 1):
            query_step(
                crel * 8 + slot, both(g1, crel, slot, K0, 128), both(g1, crel, slot, V0, 128)
            )
        return carry

    lax.fori_loop(0, 2, query_loop, 0)
    late(1)
    lax.fori_loop(2, 4, query_loop, 0)

    y_o.wait_recv()
    att_scr2 = jnp.concatenate([on_scr[128:256, :], on_scr[0:128, :]], axis=0)
    pair = (o_scr[...], att_scr2)
    att_t = jnp.concatenate(
        [
            jnp.where(i == 0, pair[0].astype(F32), pair[1].astype(F32)).T,
            jnp.where(i == 0, pair[1].astype(F32), pair[0].astype(F32)).T,
        ],
        axis=0,
    ).astype(BF16)
    y_og.wait_recv()

    def gw_part(k, cc):
        col = (z_at(k) * 2 + cc) * HD
        grads_in = jnp.concatenate(
            [
                og_buf[:, pl.ds(pl.multiple_of(i * half + col, HD), HD)],
                ogx[:, pl.ds(pl.multiple_of(col, HD), HD)],
            ],
            axis=0,
        )
        return dot_nn(att_t, grads_in)

    gw_sib = []
    for place, k in enumerate(GW_ORDER):
        gs_send[place] = gw_part(k, 1 - core).astype(BF16)
        if place % 4 == 3:
            cut = slice(place - 3, place + 1)
            n = 8 if place == 3 else 13
            gw_sib.append(
                go(remote(gs_send.at[cut], gs_recv.at[cut], y_ss.at[n], y_rs.at[n], sib_dev))
            )
    for place, k in enumerate(GW_ORDER):
        gw_acc[place] = gw_part(k, core)
    pl.semaphore_wait(hello.at[1], 1)
    att_scr[i] = o_scr[0:128, :]
    att_scr[1 - i] = on_scr[128:256, :]
    att_own = jnp.concatenate([att_scr[0], att_scr[1]], axis=1)
    width = w_hbm.shape[1] // heads_n

    def lo_copy(k):
        return remote(
            lo_send.at[k - 1],
            lo_recv.at[k - 1],
            lo_ss.at[k - 1],
            lo_rs.at[k - 1],
            {"head": lax.rem(head + k, heads_n)},
        )

    for k in list(range(1, heads_n)) + [0]:
        cols = pl.ds(pl.multiple_of(lax.rem(head + k, heads_n) * width, HD), width)
        part = dot_nn(att_own, w_buf[:, cols])
        if k:
            lo_send[k - 1] = part.astype(BF16)
            go(lo_copy(k))
        else:
            lo_own[...] = part
    late(2)

    def gw_copy(k):
        return remote(
            gw_send.at[k - 1],
            gw_recv.at[k - 1],
            gw_ss.at[k - 1],
            gw_rs.at[k - 1],
            at(i, z_at(k), core),
        )

    for place, k in enumerate(GW_ORDER):
        if place % 4 == 0:
            gw_sib[place // 4].wait_recv()
        block = gw_acc[place] + gs_recv[place].astype(F32)
        if k:
            gw_send[k - 1] = block.astype(BF16)
            go(gw_copy(k))
        else:
            gw_acc[0] = block

    for off in range(1, NZ):
        ld_copy(off).wait_recv()
    ld_sib = go(remote(ld.at[0], ld.at[1], y_ss.at[9], y_rs.at[9], sib_dev))
    lax.fori_loop(4, NZ, query_loop, 0)
    for crel in (0, 1):
        for group in (0, 1):
            query_step(
                16 + crel * 2 + group, mem_rows(crel, group, MK0), mem_rows(crel, group, MV0)
            )
    finish = []

    def give(kind, out, value):
        grads[kind] = value.astype(BF16)
        copy = pltpu.make_async_copy(grads.at[kind, 0:128], out.at[:, own_cols], out_sem.at[kind])
        copy.start()
        finish.append(copy)
        return go(
            remote(
                grads.at[kind, 128:256],
                out.at[:, own_cols],
                y_ss.at[10 + kind],
                y_rs.at[10 + kind],
                y_dev,
            )
        )

    given = [give(0, gq_out, dq_scr[...] * scale)]
    ld_sib.wait_recv()
    take_sib(1, *range(5))

    k_mine = both(g1, 0, 0, K0, 128)
    v_mine = both(g1, 0, 0, V0, 128)
    dk_scr[...] = jnp.zeros_like(dk_scr)
    dv_scr[...] = jnp.zeros_like(dv_scr)

    def key_step(crel, slot):
        queries = both(g2, crel, slot, Q0, 128)
        grad_out = both(g2, crel, slot, D0, 128)
        lse_row = ld[crel, slot, 0:1, :]
        delta_row = ld[crel, slot, 1:2, :]
        s = dot_nt(k_mine, queries) * (scale * LOG2E)
        rows = []
        for yk in (0, 1):
            row = []
            for yq in (0, 1):
                bias = jnp.where(
                    mask_ref[block_of(yq, slot, crel), own_blocks[yk]] > 0, 0.0, -jnp.inf
                )
                cut = slice(yq * 128, yq * 128 + 128)
                row.append(
                    jnp.exp2(s[yk * 128 : yk * 128 + 128, cut] + (bias - lse_row[:, cut]))
                )
            rows.append(jnp.concatenate(row, axis=1))
        p = jnp.concatenate(rows, axis=0)
        dp = dot_nt(v_mine, grad_out)
        ds = (p * (dp - delta_row)).astype(BF16)
        dv_scr[...] += dot_nn(p.astype(BF16), grad_out)
        dk_scr[...] += dot_nn(ds, queries)

    def key_steps(*slots):
        for slot in slots:
            for crel in (0, 1):
                key_step(crel, slot)

    key_steps(0, 1, 2, 3, 4)
    late(3)
    take_sib(1, 5, 6)
    key_steps(5, 6)
    take_sib(1, 7)
    key_steps(7)
    given.append(give(1, gk_out, dk_scr[...] * scale))
    given.append(give(2, gv_out, dv_scr[...]))

    result = lo_own[...]
    for k in range(1, heads_n):
        lo_copy(k).wait_recv()
        result = result + lo_recv[k - 1].astype(F32)
    lo_stage[...] = result.astype(BF16)
    copy = pltpu.make_async_copy(lo_stage, lo_out, out_sem.at[3])
    copy.start()
    finish.append(copy)
    result = gw_acc[0]
    for k in range(1, NZ):
        gw_copy(k).wait_recv()
        result = result + gw_recv[k - 1].astype(F32)
    gw_stage[...] = result.astype(BF16)
    copy = pltpu.make_async_copy(gw_stage, gw_out, out_sem.at[4])
    copy.start()
    finish.append(copy)

    for copy in given:
        copy.wait_recv()
    for copy in finish:
        copy.wait()
    for copy in started:
        copy.wait_send()


def hand_out(*refs):
    ins, outs, held, sems = refs[:5], refs[5:10], refs[10:15], refs[15]
    reads = [pltpu.make_async_copy(ins[n], held[n], sems.at[0, n]) for n in range(5)]
    writes = [pltpu.make_async_copy(held[n], outs[n], sems.at[1, n]) for n in range(5)]
    for copy in reads:
        copy.start()
    for n in range(5):
        reads[n].wait()
        writes[n].start()
    for copy in writes:
        copy.wait()


def per_device(
    queries,
    key_states,
    value_states,
    memory_keys,
    memory_values,
    memory_length,
    block_mask,
    out_weight,
    out_grad,
    *,
    heads_n,
):
    rows, cols = queries.shape
    d_model = out_weight.shape[1]
    width = d_model // heads_n
    hbm = pl.BlockSpec(memory_space=pltpu.HBM)
    smem = pl.BlockSpec(memory_space=pltpu.SMEM)
    vm = pltpu.VMEM
    dma = pltpu.SemaphoreType.DMA
    grad_shape = jax.ShapeDtypeStruct((rows, cols), BF16)
    results = pl.pallas_call(
        functools.partial(kernel, heads_n),
        out_shape=(
            jax.ShapeDtypeStruct((rows, width), BF16),
            jax.ShapeDtypeStruct((cols, HD), BF16),
            grad_shape,
            grad_shape,
            grad_shape,
        ),
        in_specs=[smem, smem] + [hbm] * 7,
        out_specs=(hbm,) * 5,
        scratch_shapes=[
            vm((2, NZ, 2, ROWS1, HD), BF16),
            vm((2, NZ, 2, ROWS2, HD), BF16),
            vm((20, 256, 256), F32),
            vm((cols, d_model), BF16),
            vm((rows, d_model), BF16),
            vm((rows, d_model // 2), BF16),
            vm((2, rows, HD), BF16),
            vm((256, HD), BF16),
            vm((256, HD), BF16),
            vm((2, rows, HD), BF16),
            vm((2, NZ, 8, 256), F32),
            vm((rows, width), F32),
            vm((max(heads_n - 1, 1), rows, width), BF16),
            vm((max(heads_n - 1, 1), rows, width), BF16),
            vm((NZ, 256, HD), BF16),
            vm((NZ, 256, HD), BF16),
            vm((NZ, 256, HD), F32),
            vm((NZ - 1, 256, HD), BF16),
            vm((NZ - 1, 256, HD), BF16),
            vm((256, HD), F32),
            vm((256, HD), F32),
            vm((256, HD), F32),
            vm((256, HD), F32),
            vm((256, HD), F32),
            vm((256, HD), F32),
            vm((3, 256, HD), BF16),
            vm((rows, width), BF16),
            vm((cols, HD), BF16),
            dma((7,)),
            dma((2, 2, 4, 2)),
            dma((2, 2, 4, 2)),
            dma((2, NZ)),
            dma((2, NZ)),
            dma((14,)),
            dma((14,)),
            dma((NZ - 1,)),
            dma((NZ - 1,)),
            dma((max(heads_n - 1, 1),)),
            dma((max(heads_n - 1, 1),)),
            dma((NZ - 1,)),
            dma((NZ - 1,)),
            dma((5,)),
            pltpu.SemaphoreType.REGULAR((2,)),
        ],
        compiler_params=pltpu.CompilerParams(
            collective_id=0, has_side_effects=True, vmem_limit_bytes=56 * 1024 * 1024
        ),
        name="attention",
    )(
        memory_length,
        block_mask,
        queries,
        key_states,
        value_states,
        memory_keys,
        memory_values,
        out_weight,
        out_grad,
    )
    return pl.pallas_call(
        hand_out,
        out_shape=tuple(jax.ShapeDtypeStruct(r.shape, r.dtype) for r in results),
        in_specs=[hbm] * 5,
        out_specs=(hbm,) * 5,
        scratch_shapes=[vm(r.shape, r.dtype) for r in results] + [dma((2, 5))],
        name="results",
    )(*results)


def solution(mesh):
    in_specs = (
        P("ctx", "head"),
        P("ctx", "head"),
        P("ctx", "head"),
        P("ctx", "head"),
        P("ctx", "head"),
        P(),
        P(),
        P("head", None),
        P("ctx", None),
    )
    out_specs = (
        P("ctx", "head"),
        P("head", "ctx"),
        P("ctx", "head"),
        P("ctx", "head"),
        P("ctx", "head"),
    )
    return jax.shard_map(
        functools.partial(per_device, heads_n=mesh.shape["head"]),
        mesh=mesh,
        in_specs=in_specs,
        out_specs=out_specs,
        check_vma=False,
    )
```

```python
import functools
import math

import jax
import jax.numpy as jnp
from jax import lax
from jax.experimental import pallas as pl
from jax.experimental.pallas import tpu as pltpu
from jax.sharding import PartitionSpec as P

HD = 128
BLK = 128
NZ = 8
NX = 4
LAG = 3
GW_ORDER = (4, 3, 5, 2, 6, 1, 7, 0)
F32 = jnp.float32
BF16 = jnp.bfloat16
MESH = pl.DeviceIdType.MESH
LOG2E = 1.4426950408889634

OFFSET = (0, -1, 1, -2, 2, -3, 3, 4)
SLOT_OF = {off % NZ: slot for slot, off in enumerate(OFFSET)}

K0, V0, MK0, MV0, ROWS1 = 0, 128, 256, 288, 320
Q0, D0, ROWS2 = 0, 128, 256


def dot_nt(a, b):
    return lax.dot_general(a, b, (((1,), (1,)), ((), ())), preferred_element_type=F32)


def dot_nn(a, b):
    return lax.dot_general(a, b, (((1,), (0,)), ((), ())), preferred_element_type=F32)


def kernel(
    heads_n,
    len_ref,
    mask_ref,
    q_hbm,
    k_hbm,
    v_hbm,
    mk_hbm,
    mv_hbm,
    w_hbm,
    og_hbm,
    lo_out,
    gw_out,
    gq_out,
    gk_out,
    gv_out,
    g1,
    g2,
    s_buf,
    w_buf,
    og_buf,
    ogx,
    do_scr,
    o_scr,
    on_scr,
    att_scr,
    ld,
    lo_own,
    lo_send,
    lo_recv,
    gs_send,
    gs_recv,
    gw_acc,
    gw_send,
    gw_recv,
    m_scr,
    l_scr,
    acc_scr,
    dq_scr,
    dk_scr,
    dv_scr,
    grads,
    lo_stage,
    gw_stage,
    local_sem,
    ring_ss,
    ring_rs,
    sib_ss,
    sib_rs,
    y_ss,
    y_rs,
    ld_ss,
    ld_rs,
    lo_ss,
    lo_rs,
    gw_ss,
    gw_rs,
    out_sem,
    hello,
):
    ctx = lax.axis_index("ctx")
    head = lax.axis_index("head")
    core = lax.rem(ctx, 2)
    z = lax.rem(ctx // 2, NZ)
    i = ctx // (2 * NZ)
    scale = 1.0 / math.sqrt(HD)

    def at(ii, zz, cc):
        return {"ctx": (ii * NZ + zz) * 2 + cc}

    def z_at(off):
        return lax.rem(z + (off % NZ), NZ)

    y_dev = at(1 - i, z, core)
    sib_dev = at(i, z, 1 - core)
    own_cols = pl.ds(pl.multiple_of(i * HD, HD), HD)
    other_cols = pl.ds(pl.multiple_of((1 - i) * HD, HD), HD)
    gather = (g1, g2)
    started = []

    def remote(src, dst, ss, rs, dev):
        return pltpu.make_async_remote_copy(
            src_ref=src, dst_ref=dst, send_sem=ss, recv_sem=rs, device_id=dev, device_id_type=MESH
        )

    def go(copy):
        copy.start()
        started.append(copy)
        return copy

    piece = g1.at[0, 0, 0]
    local1 = [
        pltpu.make_async_copy(k_hbm.at[:, own_cols], piece.at[K0 : K0 + 128], local_sem.at[0]),
        pltpu.make_async_copy(v_hbm.at[:, own_cols], piece.at[V0 : V0 + 128], local_sem.at[1]),
        pltpu.make_async_copy(mk_hbm.at[:, own_cols], piece.at[MK0 : MK0 + 32], local_sem.at[2]),
        pltpu.make_async_copy(mv_hbm.at[:, own_cols], piece.at[MV0 : MV0 + 32], local_sem.at[3]),
    ]
    local_q = pltpu.make_async_copy(
        q_hbm.at[:, own_cols], g2.at[0, 0, 0, Q0 : Q0 + 128], local_sem.at[4]
    )
    local_w = pltpu.make_async_copy(w_hbm, w_buf, local_sem.at[5])
    local_og = pltpu.make_async_copy(og_hbm, og_buf, local_sem.at[6])
    for copy in local1:
        copy.start()
    local_q.start()
    local_og.start()
    local_w.start()

    barrier = pltpu.get_barrier_semaphore()
    x = lax.rem(head, NX)
    row = head - x
    x_next = {"head": row + lax.rem(x + 1, NX)}
    x_last = {"head": row + lax.rem(x + NX - 1, NX)}
    row_dev = {"head": lax.rem(head + NX, heads_n)}
    peers = [y_dev, sib_dev, at(i, z_at(1), core), at(i, z_at(-1), core), x_next, x_last, row_dev]
    for dev in peers:
        pl.semaphore_signal(barrier, inc=1, device_id=dev, device_id_type=MESH)

    pl.semaphore_wait(barrier, len(peers))

    far = g1.at[0, 0, 1]
    y_first = [
        remote(k_hbm.at[:, other_cols], far.at[K0 : K0 + 128], y_ss.at[0], y_rs.at[0], y_dev),
        remote(v_hbm.at[:, other_cols], far.at[V0 : V0 + 128], y_ss.at[1], y_rs.at[1], y_dev),
        remote(mk_hbm.at[:, other_cols], far.at[MK0 : MK0 + 32], y_ss.at[2], y_rs.at[2], y_dev),
        remote(mv_hbm.at[:, other_cols], far.at[MV0 : MV0 + 32], y_ss.at[3], y_rs.at[3], y_dev),
    ]
    y_q = remote(
        q_hbm.at[:, other_cols], g2.at[0, 0, 1, Q0 : Q0 + 128], y_ss.at[4], y_rs.at[4], y_dev
    )

    def ring(phase, way, step, part):
        src = 0 if step == 0 else 2 * step - 1 + way
        dst = 7 if step == 3 else 2 * step + 1 + way
        buf = gather[phase]
        return remote(
            buf.at[0, src, part],
            buf.at[0, dst, part],
            ring_ss.at[phase, way, step, part],
            ring_rs.at[phase, way, step, part],
            at(i, z_at(1 if way == 0 else -1), core),
        )

    def ring_send(phase, step, part):
        for way in (0, 1):
            if step < 3 or part == way:
                go(ring(phase, way, step, part))

    def sib(phase, slot):
        buf = gather[phase]
        return remote(
            buf.at[0, slot], buf.at[1, slot], sib_ss.at[phase, slot], sib_rs.at[phase, slot], sib_dev
        )

    def follow(step):
        if step == 1:
            if LAG == 0:
                local_q.wait()
            ring_send(1, 0, 0)
            if LAG == 0:
                y_q.wait_recv()
            y_do.wait_recv()
            ring_send(1, 0, 1)
            go(sib(1, 0))
        if step >= LAG:
            advance(1, step - LAG)

    def take(phase, step, part):
        for way in (0, 1):
            ring(phase, way, step, part).wait_recv()
            if step < 2 or part == way:
                go(ring(phase, way, step + 1, part))

    def advance(phase, step):
        if step < 3:
            for part in (0, 1):
                if (phase, step, part) != (0, 0, 0):
                    take(phase, step, part)
            go(sib(phase, 2 * step + 1))
            go(sib(phase, 2 * step + 2))
        else:
            ring(phase, 0, 3, 0).wait_recv()
            ring(phase, 1, 3, 1).wait_recv()
            go(sib(phase, 7))

    for copy in local1:
        copy.wait()
    ring_send(0, 0, 0)
    for copy in y_first:
        go(copy)
    go(y_q)
    pl.semaphore_signal(hello.at[0], inc=1, device_id=x_next, device_id_type=MESH)

    local_og.wait()
    local_w.wait()
    grad_att = dot_nt(og_buf[...], w_buf[...]).astype(BF16)
    do_scr[0] = grad_att[:, :HD]
    do_scr[1] = grad_att[:, HD:]
    g2[0, 0, 0, D0 : D0 + 128, :] = do_scr[i]
    y_do = go(
        remote(do_scr.at[1 - i], g2.at[0, 0, 1, D0 : D0 + 128], y_ss.at[5], y_rs.at[5], y_dev)
    )
    take(0, 0, 0)
    for copy in y_first:
        copy.wait_recv()
    ring_send(0, 0, 1)
    go(sib(0, 0))
    half = og_hbm.shape[1] // 2
    y_og = go(
        remote(
            og_hbm.at[:, pl.ds(pl.multiple_of((1 - i) * half, HD), half)],
            ogx,
            y_ss.at[6],
            y_rs.at[6],
            y_dev,
        )
    )
    follow(-1)
    if LAG > 0:
        local_q.wait()
        y_q.wait_recv()

    def block_of(part, slot, crel):
        ii = i if part == 0 else 1 - i
        cc = core if crel == 0 else 1 - core
        return (ii * NZ + z_at(OFFSET[slot])) * 2 + cc

    own_blocks = [block_of(0, 0, 0), block_of(1, 0, 0)]

    def both(buf, crel, slot, row, rows):
        return jnp.concatenate(
            [buf[crel, slot, 0, row : row + rows, :], buf[crel, slot, 1, row : row + rows, :]], axis=0
        )

    q_mine = both(g2, 0, 0, Q0, 128)
    m_scr[...] = jnp.full_like(m_scr, -jnp.inf)
    l_scr[...] = jnp.zeros_like(l_scr)
    acc_scr[...] = jnp.zeros_like(acc_scr)
    lane = lax.broadcasted_iota(jnp.int32, (1, 256), 1)

    def seq_scores(crel, slot):
        s = dot_nt(q_mine, both(g1, crel, slot, K0, 128)) * (scale * LOG2E)
        top = None
        for yq in (0, 1):
            row = []
            for yk in (0, 1):
                bias = jnp.where(
                    mask_ref[own_blocks[yq], block_of(yk, slot, crel)] > 0, 0.0, -jnp.inf
                )
                row.append(s[yq * 128 : yq * 128 + 128, yk * 128 : yk * 128 + 128] + bias)
                s_buf[crel * 8 + slot, yq * 128 : yq * 128 + 128, yk * 128 : yk * 128 + 128] = row[yk]
            both_k = jnp.maximum(row[0], row[1])
            top = both_k if top is None else jnp.concatenate([top, both_k], axis=0)
        return top

    def mem_rows(crel, group, row):
        return jnp.concatenate(
            [
                g1[crel, slot, part, row : row + 32, :]
                for slot in range(4 * group, 4 * group + 4)
                for part in (0, 1)
            ],
            axis=0,
        )

    def mem_scores(crel, group):
        s = dot_nt(q_mine, mem_rows(crel, group, MK0)) * (scale * LOG2E)
        base = jnp.zeros((1, 256), jnp.int32)
        place = 0
        for slot in range(4 * group, 4 * group + 4):
            for part in (0, 1):
                base = jnp.where(lane // 32 == place, block_of(part, slot, crel), base)
                place += 1
        index = base * 32 + lane % 32
        top = []
        for yq in (0, 1):
            allow = index < len_ref[own_blocks[yq]]
            t = jnp.where(allow, s[yq * 128 : yq * 128 + 128, :], -jnp.inf)
            s_buf[16 + crel * 2 + group, yq * 128 : yq * 128 + 128, :] = t
            top.append(jnp.maximum(t[:, :128], t[:, 128:]))
        return jnp.concatenate(top, axis=0)

    def absorb(chunks):
        tops = [mem_scores(*c[1:]) if c[0] else seq_scores(*c[1:]) for c in chunks]
        top = functools.reduce(jnp.maximum, tops)
        old = m_scr[...]
        new = jnp.maximum(old, jnp.broadcast_to(jnp.max(top, axis=1, keepdims=True), old.shape))
        fade = jnp.exp2(old - new)
        total = l_scr[...] * fade
        accum = acc_scr[...] * fade
        for mem, crel, slot in chunks:
            j = 16 + crel * 2 + slot if mem else crel * 8 + slot
            values = mem_rows(crel, slot, MV0) if mem else both(g1, crel, slot, V0, 128)
            p = jnp.exp2(s_buf[j] - jnp.concatenate([new, new], axis=1))
            total = total + p[:, :128] + p[:, 128:]
            high = p.astype(BF16)
            low = (p - high.astype(F32)).astype(BF16)
            accum = accum + dot_nn(high, values) + dot_nn(low, values)
        m_scr[...] = new
        l_scr[...] = total
        acc_scr[...] = accum

    def late(step):
        if step > 3 - LAG:
            advance(1, step)

    def take_sib(phase, *slots):
        for slot in slots:
            sib(phase, slot).wait_recv()

    absorb([(0, 0, 0)])
    advance(0, 0)
    follow(0)
    absorb([(0, 0, 1), (0, 0, 2)])
    take_sib(0, 0)
    absorb([(0, 1, 0)])
    advance(0, 1)
    follow(1)
    pl.semaphore_wait(hello.at[0], 1)
    pl.semaphore_signal(hello.at[1], inc=1, device_id=row_dev, device_id_type=MESH)
    absorb([(0, 0, 3), (0, 0, 4)])
    take_sib(0, 1, 2)
    absorb([(0, 1, 1), (0, 1, 2)])
    advance(0, 2)
    follow(2)
    absorb([(0, 0, 5), (0, 0, 6), (1, 0, 0)])
    take_sib(0, 3, 4)
    absorb([(0, 1, 3), (0, 1, 4)])
    follow(3)
    advance(0, 3)
    absorb([(0, 0, 7), (1, 0, 1)])
    take_sib(0, 5, 6)
    absorb([(0, 1, 5), (0, 1, 6), (1, 1, 0)])
    take_sib(0, 7)
    absorb([(0, 1, 7), (1, 1, 1)])

    total = jnp.broadcast_to(jnp.sum(l_scr[...], axis=1, keepdims=True), (256, 128))
    lse = m_scr[...] + jnp.log2(total)
    attended = (acc_scr[...] / total).astype(BF16)
    o_scr[...] = attended
    y_o = go(remote(o_scr, on_scr, y_ss.at[7], y_rs.at[7], y_dev))
    do_mine = both(g2, 0, 0, D0, 128)
    delta = jnp.broadcast_to(
        jnp.sum(do_mine.astype(F32) * attended.astype(F32), axis=1, keepdims=True), (256, 128)
    )
    m_scr[...] = lse
    l_scr[...] = delta
    eye = lax.broadcasted_iota(jnp.int32, (128, 128), 0) == lax.broadcasted_iota(
        jnp.int32, (128, 128), 1
    )
    ld[0, 0] = jnp.zeros((8, 256), F32)
    for yq in (0, 1):
        rows = slice(yq * 128, yq * 128 + 128)
        ld[0, 0, 0:1, rows] = jnp.sum(jnp.where(eye, lse[rows, :], 0.0), axis=0, keepdims=True)
        ld[0, 0, 1:2, rows] = jnp.sum(jnp.where(eye, delta[rows, :], 0.0), axis=0, keepdims=True)

    def ld_copy(off):
        slot = SLOT_OF[(-off) % NZ]
        return remote(
            ld.at[0, 0], ld.at[0, slot], ld_ss.at[slot - 1], ld_rs.at[slot - 1], at(i, z_at(off), core)
        )

    for off in (4, 3, 5, 2, 6, 1, 7):
        go(ld_copy(off))
    late(0)

    dq_scr[...] = jnp.zeros_like(dq_scr)

    def query_step(j, keys, values):
        p = jnp.exp2(s_buf[j] - jnp.concatenate([m_scr[...], m_scr[...]], axis=1))
        dp = dot_nt(do_mine, values)
        ds = (p * (dp - jnp.concatenate([l_scr[...], l_scr[...]], axis=1))).astype(BF16)
        dq_scr[...] += dot_nn(ds, keys)

    def query_loop(slot, carry):
        for crel in (0, 1):
            query_step(
                crel * 8 + slot, both(g1, crel, slot, K0, 128), both(g1, crel, slot, V0, 128)
            )
        return carry

    lax.fori_loop(0, 2, query_loop, 0)
    late(1)
    lax.fori_loop(2, 4, query_loop, 0)

    y_o.wait_recv()
    att_scr2 = jnp.concatenate([on_scr[128:256, :], on_scr[0:128, :]], axis=0)
    pair = (o_scr[...], att_scr2)
    att_t = jnp.concatenate(
        [
            jnp.where(i == 0, pair[0].astype(F32), pair[1].astype(F32)).T,
            jnp.where(i == 0, pair[1].astype(F32), pair[0].astype(F32)).T,
        ],
        axis=0,
    ).astype(BF16)
    y_og.wait_recv()

    def gw_part(k, cc):
        col = (z_at(k) * 2 + cc) * HD
        grads_in = jnp.concatenate(
            [
                og_buf[:, pl.ds(pl.multiple_of(i * half + col, HD), HD)],
                ogx[:, pl.ds(pl.multiple_of(col, HD), HD)],
            ],
            axis=0,
        )
        return dot_nn(att_t, grads_in)

    gw_sib = []
    for place, k in enumerate(GW_ORDER):
        gs_send[place] = gw_part(k, 1 - core).astype(BF16)
        if place % 4 == 3:
            cut = slice(place - 3, place + 1)
            n = 8 if place == 3 else 13
            gw_sib.append(
                go(remote(gs_send.at[cut], gs_recv.at[cut], y_ss.at[n], y_rs.at[n], sib_dev))
            )
    for place, k in enumerate(GW_ORDER):
        gw_acc[place] = gw_part(k, core)
    pl.semaphore_wait(hello.at[1], 1)
    att_scr[i] = o_scr[0:128, :]
    att_scr[1 - i] = on_scr[128:256, :]
    att_own = jnp.concatenate([att_scr[0], att_scr[1]], axis=1)
    width = w_hbm.shape[1] // heads_n

    def lo_copy(k):
        return remote(
            lo_send.at[k - 1],
            lo_recv.at[k - 1],
            lo_ss.at[k - 1],
            lo_rs.at[k - 1],
            {"head": lax.rem(head + k, heads_n)},
        )

    for k in list(range(1, heads_n)) + [0]:
        cols = pl.ds(pl.multiple_of(lax.rem(head + k, heads_n) * width, HD), width)
        part = dot_nn(att_own, w_buf[:, cols])
        if k:
            lo_send[k - 1] = part.astype(BF16)
            go(lo_copy(k))
        else:
            lo_own[...] = part
    late(2)

    def gw_copy(k):
        return remote(
            gw_send.at[k - 1],
            gw_recv.at[k - 1],
            gw_ss.at[k - 1],
            gw_rs.at[k - 1],
            at(i, z_at(k), core),
        )

    for place, k in enumerate(GW_ORDER):
        if place % 4 == 0:
            gw_sib[place // 4].wait_recv()
        block = gw_acc[place] + gs_recv[place].astype(F32)
        if k:
            gw_send[k - 1] = block.astype(BF16)
            go(gw_copy(k))
        else:
            gw_acc[0] = block

    for off in range(1, NZ):
        ld_copy(off).wait_recv()
    ld_sib = go(remote(ld.at[0], ld.at[1], y_ss.at[9], y_rs.at[9], sib_dev))
    lax.fori_loop(4, NZ, query_loop, 0)
    for crel in (0, 1):
        for group in (0, 1):
            query_step(
                16 + crel * 2 + group, mem_rows(crel, group, MK0), mem_rows(crel, group, MV0)
            )
    finish = []

    def give(kind, out, value):
        grads[kind] = value.astype(BF16)
        copy = pltpu.make_async_copy(grads.at[kind, 0:128], out.at[:, own_cols], out_sem.at[kind])
        copy.start()
        finish.append(copy)
        return go(
            remote(
                grads.at[kind, 128:256],
                out.at[:, own_cols],
                y_ss.at[10 + kind],
                y_rs.at[10 + kind],
                y_dev,
            )
        )

    given = [give(0, gq_out, dq_scr[...] * scale)]
    ld_sib.wait_recv()
    take_sib(1, *range(5))

    k_mine = both(g1, 0, 0, K0, 128)
    v_mine = both(g1, 0, 0, V0, 128)
    dk_scr[...] = jnp.zeros_like(dk_scr)
    dv_scr[...] = jnp.zeros_like(dv_scr)

    def key_step(crel, slot):
        queries = both(g2, crel, slot, Q0, 128)
        grad_out = both(g2, crel, slot, D0, 128)
        lse_row = ld[crel, slot, 0:1, :]
        delta_row = ld[crel, slot, 1:2, :]
        s = dot_nt(k_mine, queries) * (scale * LOG2E)
        rows = []
        for yk in (0, 1):
            row = []
            for yq in (0, 1):
                bias = jnp.where(
                    mask_ref[block_of(yq, slot, crel), own_blocks[yk]] > 0, 0.0, -jnp.inf
                )
                cut = slice(yq * 128, yq * 128 + 128)
                row.append(
                    jnp.exp2(s[yk * 128 : yk * 128 + 128, cut] + (bias - lse_row[:, cut]))
                )
            rows.append(jnp.concatenate(row, axis=1))
        p = jnp.concatenate(rows, axis=0)
        dp = dot_nt(v_mine, grad_out)
        ds = (p * (dp - delta_row)).astype(BF16)
        dv_scr[...] += dot_nn(p.astype(BF16), grad_out)
        dk_scr[...] += dot_nn(ds, queries)

    def key_steps(*slots):
        for slot in slots:
            for crel in (0, 1):
                key_step(crel, slot)

    key_steps(0, 1, 2, 3, 4)
    late(3)
    take_sib(1, 5, 6)
    key_steps(5, 6)
    take_sib(1, 7)
    key_steps(7)
    given.append(give(1, gk_out, dk_scr[...] * scale))
    given.append(give(2, gv_out, dv_scr[...]))

    result = lo_own[...]
    for k in range(1, heads_n):
        lo_copy(k).wait_recv()
        result = result + lo_recv[k - 1].astype(F32)
    lo_stage[...] = result.astype(BF16)
    copy = pltpu.make_async_copy(lo_stage, lo_out, out_sem.at[3])
    copy.start()
    finish.append(copy)
    result = gw_acc[0]
    for k in range(1, NZ):
        gw_copy(k).wait_recv()
        result = result + gw_recv[k - 1].astype(F32)
    gw_stage[...] = result.astype(BF16)
    copy = pltpu.make_async_copy(gw_stage, gw_out, out_sem.at[4])
    copy.start()
    finish.append(copy)

    for copy in given:
        copy.wait_recv()
    for copy in finish:
        copy.wait()
    for copy in started:
        copy.wait_send()


def hand_out(*refs):
    ins, outs, held, sems = refs[:5], refs[5:10], refs[10:15], refs[15]
    reads = [pltpu.make_async_copy(ins[n], held[n], sems.at[0, n]) for n in range(5)]
    writes = [pltpu.make_async_copy(held[n], outs[n], sems.at[1, n]) for n in range(5)]
    for copy in reads:
        copy.start()
    for n in range(5):
        reads[n].wait()
        writes[n].start()
    for copy in writes:
        copy.wait()


def per_device(
    queries,
    key_states,
    value_states,
    memory_keys,
    memory_values,
    memory_length,
    block_mask,
    out_weight,
    out_grad,
    *,
    heads_n,
):
    rows, cols = queries.shape
    d_model = out_weight.shape[1]
    width = d_model // heads_n
    hbm = pl.BlockSpec(memory_space=pltpu.HBM)
    smem = pl.BlockSpec(memory_space=pltpu.SMEM)
    vm = pltpu.VMEM
    dma = pltpu.SemaphoreType.DMA
    grad_shape = jax.ShapeDtypeStruct((rows, cols), BF16)
    results = pl.pallas_call(
        functools.partial(kernel, heads_n),
        out_shape=(
            jax.ShapeDtypeStruct((rows, width), BF16),
            jax.ShapeDtypeStruct((cols, HD), BF16),
            grad_shape,
            grad_shape,
            grad_shape,
        ),
        in_specs=[smem, smem] + [hbm] * 7,
        out_specs=(hbm,) * 5,
        scratch_shapes=[
            vm((2, NZ, 2, ROWS1, HD), BF16),
            vm((2, NZ, 2, ROWS2, HD), BF16),
            vm((20, 256, 256), F32),
            vm((cols, d_model), BF16),
            vm((rows, d_model), BF16),
            vm((rows, d_model // 2), BF16),
            vm((2, rows, HD), BF16),
            vm((256, HD), BF16),
            vm((256, HD), BF16),
            vm((2, rows, HD), BF16),
            vm((2, NZ, 8, 256), F32),
            vm((rows, width), F32),
            vm((max(heads_n - 1, 1), rows, width), BF16),
            vm((max(heads_n - 1, 1), rows, width), BF16),
            vm((NZ, 256, HD), BF16),
            vm((NZ, 256, HD), BF16),
            vm((NZ, 256, HD), F32),
            vm((NZ - 1, 256, HD), BF16),
            vm((NZ - 1, 256, HD), BF16),
            vm((256, HD), F32),
            vm((256, HD), F32),
            vm((256, HD), F32),
            vm((256, HD), F32),
            vm((256, HD), F32),
            vm((256, HD), F32),
            vm((3, 256, HD), BF16),
            vm((rows, width), BF16),
            vm((cols, HD), BF16),
            dma((7,)),
            dma((2, 2, 4, 2)),
            dma((2, 2, 4, 2)),
            dma((2, NZ)),
            dma((2, NZ)),
            dma((14,)),
            dma((14,)),
            dma((NZ - 1,)),
            dma((NZ - 1,)),
            dma((max(heads_n - 1, 1),)),
            dma((max(heads_n - 1, 1),)),
            dma((NZ - 1,)),
            dma((NZ - 1,)),
            dma((5,)),
            pltpu.SemaphoreType.REGULAR((2,)),
        ],
        compiler_params=pltpu.CompilerParams(
            collective_id=0, has_side_effects=True, vmem_limit_bytes=56 * 1024 * 1024
        ),
        name="attention",
    )(
        memory_length,
        block_mask,
        queries,
        key_states,
        value_states,
        memory_keys,
        memory_values,
        out_weight,
        out_grad,
    )
    return pl.pallas_call(
        hand_out,
        out_shape=tuple(jax.ShapeDtypeStruct(r.shape, r.dtype) for r in results),
        in_specs=[hbm] * 5,
        out_specs=(hbm,) * 5,
        scratch_shapes=[vm(r.shape, r.dtype) for r in results] + [dma((2, 5))],
        name="results",
    )(*results)


def solution(mesh):
    in_specs = (
        P("ctx", "head"),
        P("ctx", "head"),
        P("ctx", "head"),
        P("ctx", "head"),
        P("ctx", "head"),
        P(),
        P(),
        P("head", None),
        P("ctx", None),
    )
    out_specs = (
        P("ctx", "head"),
        P("head", "ctx"),
        P("ctx", "head"),
        P("ctx", "head"),
        P("ctx", "head"),
    )
    return jax.shard_map(
        functools.partial(per_device, heads_n=mesh.shape["head"]),
        mesh=mesh,
        in_specs=in_specs,
        out_specs=out_specs,
        check_vma=False,
    )
```
